32 devices in a mesh: row: 4 (over y, x), col: 8 (over z, core).
Axes of the slice: x: 2, y: 2, z: 4, core: 2. Of those that a mesh axis runs over, the one named last changes fastest.
Arguments:
- features: bfloat16 [8192, 128], P(('row', 'col')), may hold values from -3 to 3
- weight: bfloat16 [128, 128], replicated, may hold values from -0.5 to 0.5
- cuts: int32 [32, 8], P(('row', 'col')), may hold values from 0 to 255
- pos_rows: int32 [4, 8, 384], P('row', 'col'), may hold values from 0 to 15
- pos_cols: int32 [4, 8, 384], P('row', 'col'), may hold values from 0 to 7
- pos_keys: int32 [4, 8, 384], P('row', 'col'), may hold values from 0 to 1073741823
- pos_count: int32 [4, 8], P('row', 'col'), may hold values from 96 to 384, as said below
- neg_rows: int32 [4, 8, 128], P('row', 'col'), may hold values from 0 to 15
- neg_cols: int32 [4, 8, 128], P('row', 'col'), may hold values from 0 to 7
Outputs:
- grad_features: bfloat16 [8192, 128], P(('row', 'col'))
- grad_weight: float32 [128, 128], replicated
The draws below stay inside these ranges and needn't reach their ends.
Inputs may be any that keep to these rules, and one draw needn't show every extreme that they name: `pos_count`: one tile in every draw has all 384 slots live.
All inputs are finite; a program needn't handle non-finite values.
Results may differ from the reference program's by a relative error of at most 0.0053.
Values may be sent and summed in bfloat16 or wider, within the bound.
No kernel may reach another device: no remote copies, remote signals or barrier semaphores. Data moves between devices by JAX's collectives and lax.ppermute only.
A program may use at most 64 MiB of HBM per device.

```python
import jax
import jax.numpy as jnp
from jax import lax

LAT = 128
FEAT = 128
BLOCK = 128
CUTS = 8
NODE_DEV = 256
POS_PAIRS = 384
NEG_PAIRS = 128
SHARDS = 32
NODES = 8192
ROW_BLOCKS = 16
COL_BLOCKS = 8
N_ROW = 4
N_COL = 8


def draw_pos_count(key, part):
    key = jax.random.fold_in(key, 7)
    first, second = jax.random.split(key)
    counts = jax.random.randint(first, (N_ROW * N_COL,), POS_PAIRS // 4, POS_PAIRS + 1)
    spot = jax.random.randint(second, (), 0, N_ROW * N_COL)
    filled = jnp.where(jnp.arange(N_ROW * N_COL) == spot, POS_PAIRS, counts)
    return filled.reshape(N_ROW, N_COL).astype(jnp.int32)


def set_ends(array, rng, least, largest):
    longest = array.shape.index(max(array.shape))
    spots = []
    for shift in (0, 1):
        where = [jax.random.randint(jax.random.fold_in(rng, axis), (), 0, length) for axis, length in enumerate(array.shape)]
        where[longest] = (where[longest] + shift) % array.shape[longest]
        spots.append(tuple(where))
    return array.at[spots[0]].set(least).at[spots[1]].set(largest)


def block_levels(own_key, shape, cuts, low, high):
    loudness, own = 1.0, jax.random.fold_in(own_key, 6)
    for position, blocks in cuts:
        draws = jnp.exp(jax.random.uniform(jax.random.fold_in(own, position), (blocks,), jnp.float32, low / len(cuts), high / len(cuts)))
        loudness = loudness * jnp.repeat(draws, shape[position] // blocks).reshape([-1 if axis == position else 1 for axis in range(len(shape))])
    return loudness


def bell_draw(rng, shape, spread, bound, pieces=(), kind=jnp.bfloat16):
    gain = block_levels(rng, shape, pieces, -0.22, 0.18) if pieces else 1.0
    entries = jax.random.normal(rng, shape, jnp.float32) * spread * gain
    return jnp.minimum(jnp.maximum(entries, -bound), bound).astype(kind)


def setup_inputs(seed: int = 0) -> dict:
    arg_keys = jax.random.split(jax.random.key(seed), 10)
    return {
        "features": bell_draw(arg_keys[0], (NODES, FEAT), 0.5, 3.0, ((0, 32),)),
        "weight": bell_draw(arg_keys[1], (FEAT, LAT), FEAT ** -0.5, 0.5),
        "cuts": set_ends(jax.random.randint(arg_keys[2], (SHARDS, CUTS), 0, NODE_DEV), jax.random.fold_in(arg_keys[2], 1), 0, NODE_DEV - 1).astype(jnp.int32),
        "pos_rows": set_ends(jax.random.randint(arg_keys[3], (N_ROW, N_COL, POS_PAIRS), 0, ROW_BLOCKS), jax.random.fold_in(arg_keys[3], 1), 0, ROW_BLOCKS - 1).astype(jnp.int32),
        "pos_cols": set_ends(jax.random.randint(arg_keys[4], (N_ROW, N_COL, POS_PAIRS), 0, COL_BLOCKS), jax.random.fold_in(arg_keys[4], 1), 0, COL_BLOCKS - 1).astype(jnp.int32),
        "pos_keys": set_ends(jax.random.randint(arg_keys[5], (N_ROW, N_COL, POS_PAIRS), 0, 1073741824), jax.random.fold_in(arg_keys[5], 1), 0, 1073741823).astype(jnp.int32),
        "pos_count": draw_pos_count(jax.random.fold_in(arg_keys[9], 71), 0),
        "neg_rows": set_ends(jax.random.randint(arg_keys[7], (N_ROW, N_COL, NEG_PAIRS), 0, ROW_BLOCKS), jax.random.fold_in(arg_keys[7], 1), 0, ROW_BLOCKS - 1).astype(jnp.int32),
        "neg_cols": set_ends(jax.random.randint(arg_keys[8], (N_ROW, N_COL, NEG_PAIRS), 0, COL_BLOCKS), jax.random.fold_in(arg_keys[8], 1), 0, COL_BLOCKS - 1).astype(jnp.int32),
    }


def edge_targets(keys, size):
    first = lax.broadcasted_iota(jnp.int32, (size, size), 0)
    second = lax.broadcasted_iota(jnp.int32, (size, size), 1)
    hashed = (keys[:, None, None] + 40503 * (size * first + second)[None]) % 1073741824
    mixed = jnp.right_shift(jnp.bitwise_xor(hashed, jnp.right_shift(hashed, 11)), 7)
    return (mixed % 5 == 0).astype(jnp.float32)


def operator_apply(values, link):
    values = values.astype(jnp.float32)
    link_f = link.astype(jnp.float32)[:, None]
    linked = link_f * values
    zero_row = jnp.zeros((1, values.shape[1]), jnp.float32)
    before = jnp.concatenate([zero_row, values[:-1]], axis=0)
    after = jnp.concatenate([linked[1:], zero_row], axis=0)
    return 0.5 * values + 0.25 * (link_f * before + after)


def reference(features, weight, cuts, pos_rows, pos_cols, pos_keys, pos_count, neg_rows, neg_cols):
    offsets = lax.broadcasted_iota(jnp.int32, (SHARDS, CUTS, NODE_DEV), 2)
    hit = jnp.any(cuts[:, :, None] == offsets, axis=1)
    link = (1 - hit.astype(jnp.int32)).reshape(NODES)
    agg = operator_apply(features, link).astype(jnp.bfloat16)
    latent = jnp.dot(agg, weight, preferred_element_type=jnp.float32).astype(jnp.bfloat16)
    grid = latent.reshape(N_ROW, N_COL, NODE_DEV, LAT)
    total_pairs = POS_PAIRS + NEG_PAIRS
    rows_all = jnp.concatenate([pos_rows, neg_rows], axis=2).reshape(SHARDS, total_pairs)
    cols_all = jnp.concatenate([pos_cols, neg_cols], axis=2).reshape(SHARDS, total_pairs)
    keys_all = pos_keys.reshape(SHARDS, POS_PAIRS)
    counts = pos_count.reshape(SHARDS)

    def tile(grads, inputs):
        index, rows, cols, keys, count = inputs
        rank_r = index // N_COL
        rank_c = index % N_COL
        row_z = lax.dynamic_index_in_dim(grid, rank_r, 0, keepdims=False).reshape(ROW_BLOCKS, BLOCK, LAT)
        col_z = lax.dynamic_index_in_dim(grid, rank_c, 1, keepdims=False).reshape(COL_BLOCKS, BLOCK, LAT)
        near = jnp.take(row_z, rows, axis=0).astype(jnp.float32)
        far = jnp.take(col_z, cols, axis=0).astype(jnp.float32)
        logits = jnp.einsum('gal,gbl->gab', near, far)
        targets = jnp.concatenate([edge_targets(keys, BLOCK), jnp.zeros((NEG_PAIRS, BLOCK, BLOCK), jnp.float32)], axis=0)
        slots = lax.broadcasted_iota(jnp.int32, (total_pairs,), 0)
        live = jnp.where(slots < POS_PAIRS, (slots < count).astype(jnp.float32), 1.0)
        pair_grad = ((jax.nn.sigmoid(logits) - targets) * (live[:, None, None] / 32.0)).astype(jnp.bfloat16).astype(jnp.float32)
        row_terms = jnp.einsum('gab,gbl->gal', pair_grad, far)
        col_terms = jnp.einsum('gab,gal->gbl', pair_grad, near)
        row_part = jax.ops.segment_sum(row_terms, rows, num_segments=ROW_BLOCKS)
        col_part = jax.ops.segment_sum(col_terms, cols, num_segments=COL_BLOCKS)
        grads = grads.at[rank_r].add(row_part.reshape(N_COL, NODE_DEV, LAT))
        grads = grads.at[:, rank_c].add(col_part.reshape(N_ROW, NODE_DEV, LAT))
        return grads, None

    start = jnp.zeros((N_ROW, N_COL, NODE_DEV, LAT), jnp.float32)
    indices = lax.broadcasted_iota(jnp.int32, (SHARDS,), 0)
    grads, _ = lax.scan(tile, start, (indices, rows_all, cols_all, keys_all, counts))
    dlatent = grads.reshape(NODES, LAT).astype(jnp.bfloat16)
    grad_weight = lax.dot_general(agg, dlatent, (((0,), (0,)), ((), ())), preferred_element_type=jnp.float32) * (NODES ** -0.5)
    dagg = lax.dot_general(dlatent, weight, (((1,), (1,)), ((), ())), preferred_element_type=jnp.float32).astype(jnp.bfloat16)
    grad_features = operator_apply(dagg, link).astype(jnp.bfloat16)
    return grad_features, grad_weight
```

```python
import functools

import jax
import jax.numpy as jnp
from jax import lax
from jax.experimental import pallas as pl
from jax.experimental.pallas import tpu as pltpu
from jax.sharding import PartitionSpec as P

BLOCK = 128
AXES = ("row", "col")
INV5 = -858993459
ANY = pl.BlockSpec(memory_space=pl.ANY)
VMEM = pl.BlockSpec(memory_space=pltpu.VMEM)
SMEM = pl.BlockSpec(memory_space=pltpu.SMEM)
CHUNK_CELLS = 128


def params(mib):
    return pltpu.CompilerParams(vmem_limit_bytes=mib * 2**20)


def swap(x, axis, step):
    count = lax.axis_size(axis)
    return lax.ppermute(x, axis, [(i, i ^ step) for i in range(count)])


def swap_next(x):
    count = lax.axis_size("row") * lax.axis_size("col")
    pairs = []
    for s in range(1, count - 1, 2):
        pairs += [(s, s + 1), (s + 1, s)]
    return lax.ppermute(x, AXES, pairs)


def links(cuts_ref, rows, width):
    node = lax.broadcasted_iota(jnp.int32, (rows, width), 0)
    cut = node == cuts_ref[0, 0]
    for t in range(1, cuts_ref.shape[1]):
        cut = jnp.logical_or(cut, node == cuts_ref[0, t])
    return jnp.where(cut, 0.0, 1.0).astype(jnp.float32)


def edges(values, link, out_ref):
    rows, width = values.shape
    head = link[0:8] * values[0:8]
    tail = values[rows - 8 : rows]
    out_ref[...] = jnp.concatenate([head, tail], axis=0).astype(out_ref.dtype)


def stencil(values, link, near_ref, far_ref):
    rows, width = values.shape
    odd = lax.rem(lax.axis_index("col"), 2) == 1
    near = near_ref[...].astype(jnp.float32)
    far = far_ref[...].astype(jnp.float32)
    prev = jnp.where(odd, near[15:16], far[15:16])
    nxt = jnp.where(odd, far[0:1], near[0:1])
    node = lax.broadcasted_iota(jnp.int32, (rows, width), 0)
    before = jnp.where(node == 0, prev, pltpu.roll(values, 1, 0))
    after = jnp.where(node == rows - 1, nxt, pltpu.roll(link * values, rows - 1, 0))
    return 0.5 * values + 0.25 * (link * before + after)


def edge_kernel(cuts_ref, features_ref, out_ref):
    values = features_ref[...].astype(jnp.float32)
    edges(values, links(cuts_ref, *values.shape), out_ref)


def agg_kernel(cuts_ref, features_ref, near_ref, far_ref, out_ref):
    values = features_ref[...].astype(jnp.float32)
    link = links(cuts_ref, *values.shape)
    out_ref[...] = stencil(values, link, near_ref, far_ref).astype(out_ref.dtype)


def target_kernel(
    base, blocks, cols, per, filtered,
    rows_hbm, cols_hbm, keys_hbm, count_hbm, nrows_hbm, ncols_hbm,
    t_hbm, n_hbm,
    rows_s, cols_s, keys_s, count_s, nrows_s, ncols_s, npos_s, n_s,
    acc, step_ref, out, sems, osems,
):
    pairs = [
        (rows_hbm, rows_s), (cols_hbm, cols_s), (keys_hbm, keys_s),
        (count_hbm, count_s), (nrows_hbm, nrows_s), (ncols_hbm, ncols_s),
    ]
    copies = [pltpu.make_async_copy(a, b, sems.at[t]) for t, (a, b) in enumerate(pairs)]
    for copy in copies:
        copy.start()
    a = lax.broadcasted_iota(jnp.int32, (BLOCK, BLOCK), 0)
    b = lax.broadcasted_iota(jnp.int32, (BLOCK, BLOCK), 1)
    step_ref[...] = (a * BLOCK + b) * jnp.int32(4 * 40503)

    def clear(i, _):
        at = pl.multiple_of(i * BLOCK, BLOCK)
        acc[pl.ds(at, BLOCK), :] = jnp.zeros((BLOCK, cols * BLOCK), jnp.float32)
        return 0

    lax.fori_loop(0, blocks, clear, 0)
    for t in range(blocks * cols):
        npos_s[t] = 0
        n_s[0, t] = 0
    for copy in copies:
        copy.wait()
    here_rows = per * lax.axis_index("col")
    here_cols = per * lax.axis_index("row")
    count = count_s[0, 0]
    slots = rows_s.shape[2]
    unroll = 4 if slots % 4 == 0 else 1

    def place(i, j):
        return jnp.bitwise_xor(i, here_rows) - base, jnp.bitwise_xor(j, here_cols)

    def positive(s):
        i, j = place(rows_s[0, 0, s], cols_s[0, 0, s])
        key = keys_s[0, 0, s] * 4
        live = s < count

        def add():
            row = pl.multiple_of(i * BLOCK, BLOCK)
            col = pl.multiple_of(j * BLOCK, BLOCK)
            mixed = step_ref[...] + key
            mixed = jnp.bitwise_xor(
                lax.shift_right_logical(mixed, 9), lax.shift_right_logical(mixed, 20)
            )
            fifth = mixed * jnp.int32(INV5) + jnp.int32(-(2**31))
            hit = fifth < jnp.int32(-(2**31) + 2**21)
            one = jnp.where(live, 1.0, 0.0).astype(jnp.float32)
            acc[pl.ds(row, BLOCK), pl.ds(col, BLOCK)] += jnp.where(hit, one, 0.0)
            npos_s[i * cols + j] += jnp.where(live, 1, 0)

        if filtered:
            pl.when(jnp.logical_and(i >= 0, i < blocks))(add)
        else:
            add()

    def positives(g, _):
        for u in range(unroll):
            positive(g * unroll + u)
        return 0

    lax.fori_loop(0, (count + unroll - 1) // unroll, positives, 0)

    def negative(s, _):
        i, j = place(nrows_s[0, 0, s], ncols_s[0, 0, s])

        def add():
            n_s[0, i * cols + j] += 1

        if filtered:
            pl.when(jnp.logical_and(i >= 0, i < blocks))(add)
        else:
            add()
        return 0

    lax.fori_loop(0, nrows_s.shape[2], negative, 0)

    def finish(i, _):
        at = pl.multiple_of(i * BLOCK, BLOCK)
        for j in range(cols):
            half = lax.shift_right_logical(npos_s[i * cols + j], 1).astype(jnp.float32)
            tile = acc[pl.ds(at, BLOCK), pl.ds(j * BLOCK, BLOCK)]
            out[pl.ds(at, BLOCK), pl.ds(j * BLOCK, BLOCK)] = (half - tile).astype(out.dtype)
        pltpu.make_async_copy(
            out.at[pl.ds(at, BLOCK), :], t_hbm.at[pl.ds(at, BLOCK), :], osems.at[i]
        ).start()
        return 0

    lax.fori_loop(0, blocks, finish, 0)

    def total(t, _):
        n_s[0, blocks * cols + t] = n_s[0, t] + lax.bitwise_and(npos_s[t], 1)
        n_s[0, t] += npos_s[t]
        return 0

    lax.fori_loop(0, blocks * cols, total, 0)
    ncopy = pltpu.make_async_copy(n_s, n_hbm, sems.at[0])
    ncopy.start()

    def drain(i, _):
        at = pl.multiple_of(i * BLOCK, BLOCK)
        pltpu.make_async_copy(
            out.at[pl.ds(at, BLOCK), :], t_hbm.at[pl.ds(at, BLOCK), :], osems.at[i]
        ).wait()
        return 0

    lax.fori_loop(0, blocks, drain, 0)
    ncopy.wait()


def targets(base, blocks, cols, per, filtered, slots):
    smem = [pltpu.SMEM(x.shape, x.dtype) for x in slots]
    cells = blocks * cols
    return pl.pallas_call(
        functools.partial(target_kernel, base, blocks, cols, per, filtered),
        out_shape=(
            jax.ShapeDtypeStruct((blocks * BLOCK, cols * BLOCK), jnp.bfloat16),
            jax.ShapeDtypeStruct((1, 2 * cells), jnp.int32),
        ),
        in_specs=[ANY] * 6,
        out_specs=(ANY, ANY),
        scratch_shapes=smem
        + [
            pltpu.SMEM((cells,), jnp.int32),
            pltpu.SMEM((1, 2 * cells), jnp.int32),
            pltpu.VMEM((blocks * BLOCK, cols * BLOCK), jnp.float32),
            pltpu.VMEM((BLOCK, BLOCK), jnp.int32),
            pltpu.VMEM((blocks * BLOCK, cols * BLOCK), jnp.bfloat16),
            pltpu.SemaphoreType.DMA((6,)),
            pltpu.SemaphoreType.DMA((blocks,)),
        ],
        compiler_params=params(40),
        cost_estimate=pl.CostEstimate(
            flops=slots[0].shape[2] * BLOCK * BLOCK * 10,
            bytes_accessed=cells * BLOCK * BLOCK * 8,
            transcendentals=0,
        ),
    )(*slots)


def decode_kernel(row_parts, col_parts, refs):
    refs = list(refs)
    t_hbm, n_hbm, weight_ref = refs[:3]
    row_refs = refs[3 : 3 + len(row_parts)]
    col_refs = refs[3 + len(row_parts) : 3 + len(row_parts) + len(col_parts)]
    rest = refs[3 + len(row_parts) + len(col_parts) :]
    drow_refs = rest[: len(row_parts)]
    dcol_refs = rest[len(row_parts) : len(row_parts) + len(col_parts)]
    share_ref, t_ref, n_s, row_z, col_z, col_acc, tsems, nsem = rest[
        len(row_parts) + len(col_parts) :
    ]
    shard = col_refs[0].shape[0]
    nrow = row_z.shape[0] // shard
    ncol = col_z.shape[0] // shard
    per = shard // BLOCK
    cols = ncol * per
    cells = nrow * per * cols

    def t_copy(p):
        at = pl.ds(p * shard, shard)
        return pltpu.make_async_copy(t_hbm.at[at, :], t_ref.at[at, :], tsems.at[p])

    ncopy = pltpu.make_async_copy(n_hbm, n_s, nsem)
    ncopy.start()
    for p in range(nrow):
        t_copy(p).start()
    weight = weight_ref[...]
    dots = functools.partial(lax.dot_general, preferred_element_type=jnp.float32)
    nn = (((1,), (0,)), ((), ()))
    nt = (((1,), (1,)), ((), ()))
    tn = (((0,), (0,)), ((), ()))
    at = 0
    for ref in col_refs:
        rows = ref.shape[0]
        col_z[at : at + rows, :] = dots(ref[...], weight, nn).astype(jnp.bfloat16)
        at += rows
    at = 0
    for ref in row_refs:
        rows = ref.shape[0]
        row_z[at : at + rows, :] = dots(ref[...], weight, nn).astype(jnp.bfloat16)
        at += rows
    ncopy.wait()
    share = jnp.zeros(share_ref.shape, jnp.float32)
    spots = [(ref, out, t) for ref, out in zip(row_refs, drow_refs) for t in range(ref.shape[0] // shard)]
    for p, (row_ref, drow_ref, t) in enumerate(spots):
        t_copy(p).wait()
        near = row_z[p * shard : (p + 1) * shard, :]
        half = near * jnp.bfloat16(0.5)
        drow = None
        for q in range(ncol):
            far = col_z[q * shard : (q + 1) * shard, :]
            curve = jnp.tanh(dots(half, far, nt))
            bands = []
            for i in range(per):
                line = []
                for j in range(per):
                    cell = (p * per + i) * cols + q * per + j
                    n = 0.5 * n_s[0, cell].astype(jnp.float32)
                    lift = 0.5 * n_s[0, cells + cell].astype(jnp.float32)
                    part = curve[i * BLOCK : (i + 1) * BLOCK, j * BLOCK : (j + 1) * BLOCK]
                    row = p * shard + i * BLOCK
                    col = q * shard + j * BLOCK
                    tile = t_ref[row : row + BLOCK, col : col + BLOCK].astype(jnp.float32)
                    line.append((n * part + (tile + lift)).astype(jnp.bfloat16))
                bands.append(jnp.concatenate(line, axis=1))
            grad = jnp.concatenate(bands, axis=0)
            term = dots(grad, far, nn)
            drow = term if drow is None else drow + term
            back = dots(grad, near, tn)
            if p == 0:
                col_acc[q * shard : (q + 1) * shard, :] = back
            else:
                col_acc[q * shard : (q + 1) * shard, :] += back
        rounded = (drow * (1.0 / 32.0)).astype(jnp.bfloat16)
        drow_ref[t * shard : (t + 1) * shard, :] = rounded
        share += dots(row_ref[t * shard : (t + 1) * shard, :], rounded, tn)
    for q in range(ncol):
        rounded = (col_acc[q * shard : (q + 1) * shard, :] * (1.0 / 32.0)).astype(jnp.bfloat16)
        dcol_refs[q][...] = rounded
        share += dots(col_refs[q][...], rounded, tn)
    share_ref[...] = share.astype(share_ref.dtype)


def decode(t, n, weight, row_parts, col_parts):
    shard = col_parts[0].shape[0]
    nrow = sum(x.shape[0] for x in row_parts) // shard
    ncol = len(col_parts)
    width = weight.shape[1]
    outs = [jax.ShapeDtypeStruct(x.shape, jnp.bfloat16) for x in row_parts + col_parts]
    outs.append(jax.ShapeDtypeStruct((weight.shape[0], width), jnp.bfloat16))
    result = pl.pallas_call(
        lambda *refs: decode_kernel(row_parts, col_parts, refs),
        out_shape=outs,
        in_specs=[ANY, ANY] + [VMEM] * (1 + len(row_parts) + len(col_parts)),
        out_specs=[VMEM] * len(outs),
        scratch_shapes=[
            pltpu.VMEM(t.shape, t.dtype),
            pltpu.SMEM(n.shape, n.dtype),
            pltpu.VMEM((nrow * shard, width), jnp.bfloat16),
            pltpu.VMEM((ncol * shard, width), jnp.bfloat16),
            pltpu.VMEM((ncol * shard, width), jnp.float32),
            pltpu.SemaphoreType.DMA((nrow,)),
            pltpu.SemaphoreType.DMA,
        ],
        compiler_params=params(40),
        cost_estimate=pl.CostEstimate(
            flops=6 * t.shape[0] * t.shape[1] * width,
            bytes_accessed=t.shape[0] * t.shape[1] * 2,
            transcendentals=t.shape[0] * t.shape[1],
        ),
    )(t, n, weight, *row_parts, *col_parts)
    return result[: len(row_parts)], result[len(row_parts) : -1], result[-1]


def latent_kernel(count, cuts_ref, weight_ref, *refs):
    parts = refs[:count]
    dagg_ref, edge_ref = refs[count:]
    total = parts[0][...].astype(jnp.float32)
    for part in parts[1:]:
        total += part[...].astype(jnp.float32)
    dlatent = total.astype(jnp.bfloat16)
    dagg = lax.dot_general(
        dlatent, weight_ref[...], (((1,), (1,)), ((), ())), preferred_element_type=jnp.float32
    ).astype(jnp.bfloat16)
    dagg_ref[...] = dagg
    values = dagg.astype(jnp.float32)
    edges(values, links(cuts_ref, *values.shape), edge_ref)


def f32(x):
    return x.astype(jnp.float32)


def tree_sum(parts):
    parts = [f32(x) for x in parts]
    while len(parts) > 1:
        parts = [a + b for a, b in zip(parts[::2], parts[1::2])]
    return parts[0]


def local(features, weight, cuts, pos_rows, pos_cols, pos_keys, pos_count, neg_rows, neg_cols):
    shard, width = features.shape
    ncol = lax.axis_size("col")
    nrow = lax.axis_size("row")
    half = ncol // 2
    per = shard // BLOCK
    message = jax.ShapeDtypeStruct((16, width), jnp.bfloat16)
    ends = pl.pallas_call(
        edge_kernel, out_shape=message, in_specs=[SMEM, VMEM], out_specs=VMEM
    )(cuts, features)
    near, far = swap(ends, "col", 1), swap_next(ends)
    slots = (pos_rows, pos_cols, pos_keys, pos_count, neg_rows, neg_cols)
    cols = nrow * per
    pieces = max(1, ncol * per * cols // CHUNK_CELLS)
    blocks = ncol * per // pieces
    found = [targets(k * blocks, blocks, cols, per, pieces > 1, slots) for k in range(pieces)]
    agg = pl.pallas_call(
        agg_kernel,
        out_shape=jax.ShapeDtypeStruct(features.shape, jnp.bfloat16),
        in_specs=[SMEM, VMEM, VMEM, VMEM],
        out_specs=VMEM,
    )(cuts, features, near, far)
    mine = [agg] + [swap(agg, "col", 2 * k) for k in range(1, half)]
    col_parts = [agg] + [swap(agg, "row", k) for k in range(1, nrow)]
    stacked = jnp.concatenate(mine, axis=0)
    theirs = swap(stacked, "col", 1)
    ordered = [x for k in range(half) for x in (mine[k], theirs[k * shard : (k + 1) * shard])]
    per_piece = blocks // per
    drow, dcols, shares = [], [], []
    for k, (t, n) in enumerate(found):
        out_rows, out_cols, share = decode(
            t, n, weight, ordered[k * per_piece : (k + 1) * per_piece], col_parts
        )
        drow += out_rows
        dcols.append(out_cols)
        shares.append(share)
    dcol = dcols[0] if pieces == 1 else [tree_sum(x).astype(jnp.bfloat16) for x in zip(*dcols)]
    share = shares[0] if pieces == 1 else tree_sum(shares).astype(jnp.bfloat16)
    send = jnp.concatenate(drow[1::2] + [share], axis=0)
    got = swap(send, "col", 1)
    kept = [
        (f32(drow[2 * k]) + f32(got[k * shard : (k + 1) * shard])).astype(jnp.bfloat16)
        for k in range(half)
    ]
    share = (f32(share) + f32(got[half * shard :])).astype(jnp.bfloat16)
    arrived = [kept[0]] + [swap(kept[k], "col", 2 * k) for k in range(1, half)]
    arrived += [dcol[0]] + [swap(dcol[k], "row", k) for k in range(1, nrow)]
    share = tree_sum([share] + [swap(share, "row", k) for k in range(1, nrow)]).astype(jnp.bfloat16)
    dagg, dends = pl.pallas_call(
        functools.partial(latent_kernel, len(arrived)),
        out_shape=(jax.ShapeDtypeStruct(features.shape, jnp.bfloat16), message),
        in_specs=[SMEM, VMEM] + [VMEM] * len(arrived),
        out_specs=(VMEM, VMEM),
    )(cuts, weight, *arrived)
    near, far = swap(dends, "col", 1), swap_next(dends)
    share = tree_sum([share] + [swap(share, "col", 2 * k) for k in range(1, half)])
    grad_features = pl.pallas_call(
        agg_kernel,
        out_shape=jax.ShapeDtypeStruct(features.shape, jnp.bfloat16),
        in_specs=[SMEM, VMEM, VMEM, VMEM],
        out_specs=VMEM,
    )(cuts, dagg, near, far)
    grad_weight = share * (shard * ncol * nrow) ** (-0.5)
    return (grad_features, grad_weight)


def solution(mesh):
    placed = (
        P(AXES, None),
        P(),
        P(AXES, None),
        P("row", "col", None),
        P("row", "col", None),
        P("row", "col", None),
        P("row", "col"),
        P("row", "col", None),
        P("row", "col", None),
    )
    return jax.shard_map(
        local, mesh=mesh, in_specs=placed, out_specs=(P(AXES, None), P()), check_vma=False
    )
```

```python
import functools

import jax
import jax.numpy as jnp
from jax import lax
from jax.experimental import pallas as pl
from jax.experimental.pallas import tpu as pltpu
from jax.sharding import PartitionSpec as P

BLOCK = 128
AXES = ("row", "col")
INV5 = -858993459
ANY = pl.BlockSpec(memory_space=pl.ANY)
VMEM = pl.BlockSpec(memory_space=pltpu.VMEM)
HBM = pl.BlockSpec(memory_space=pltpu.HBM)
SMEM = pl.BlockSpec(memory_space=pltpu.SMEM)
CHUNK_CELLS = 128
PARTS = 3


def params(mib):
    return pltpu.CompilerParams(vmem_limit_bytes=mib * 2**20)


def swap(x, axis, step):
    count = lax.axis_size(axis)
    return lax.ppermute(x, axis, [(i, i ^ step) for i in range(count)])


def swap_next(x):
    count = lax.axis_size("row") * lax.axis_size("col")
    pairs = []
    for s in range(1, count - 1, 2):
        pairs += [(s, s + 1), (s + 1, s)]
    return lax.ppermute(x, AXES, pairs)


def swap_mixed(x, step):
    nrow, ncol = lax.axis_size("row"), lax.axis_size("col")
    pairs = []
    for r in range(nrow):
        for c in range(ncol):
            if c % 2 == 0 and step < ncol // 2:
                pairs.append((r * ncol + c, r * ncol + (c ^ (2 * step))))
            if c % 2 == 1 and step < nrow:
                pairs.append((r * ncol + c, (r ^ step) * ncol + c))
    return lax.ppermute(x, AXES, pairs)


def links(cuts_ref, rows, width):
    node = lax.broadcasted_iota(jnp.int32, (rows, width), 0)
    cut = node == cuts_ref[0, 0]
    for t in range(1, cuts_ref.shape[1]):
        cut = jnp.logical_or(cut, node == cuts_ref[0, t])
    return jnp.where(cut, 0.0, 1.0).astype(jnp.float32)


def edges(values, link, out_ref):
    rows, width = values.shape
    head = link[0:8] * values[0:8]
    tail = values[rows - 8 : rows]
    out_ref[...] = jnp.concatenate([head, tail], axis=0).astype(out_ref.dtype)


def stencil(values, link, prev, nxt):
    rows, width = values.shape
    node = lax.broadcasted_iota(jnp.int32, (rows, width), 0)
    before = jnp.where(node == 0, prev, pltpu.roll(values, 1, 0))
    after = jnp.where(node == rows - 1, nxt, pltpu.roll(link * values, rows - 1, 0))
    return 0.5 * values + 0.25 * (link * before + after)


def edge_kernel(cuts_ref, features_ref, out_ref):
    values = features_ref[...].astype(jnp.float32)
    edges(values, links(cuts_ref, *values.shape), out_ref)


def pair_kernel(cuts_ref, sib_cuts_ref, features_ref, sib_ref, far_ref, sib_far_ref, out_ref):
    shard = features_ref.shape[0]

    def both(first_cuts, second_cuts, first_ref, second_ref, before_ref, after_ref):
        first = first_ref[...].astype(jnp.float32)
        second = second_ref[...].astype(jnp.float32)
        first_link = links(first_cuts, *first.shape)
        second_link = links(second_cuts, *second.shape)
        prev = before_ref[...].astype(jnp.float32)[15:16]
        nxt = after_ref[...].astype(jnp.float32)[0:1]
        head = second_link[0:1] * second[0:1]
        tail = first[shard - 1 : shard]
        out_ref[0:shard, :] = stencil(first, first_link, prev, head).astype(out_ref.dtype)
        out_ref[shard:, :] = stencil(second, second_link, tail, nxt).astype(out_ref.dtype)

    odd = lax.rem(lax.axis_index("col"), 2)

    @pl.when(odd == 0)
    def _():
        both(cuts_ref, sib_cuts_ref, features_ref, sib_ref, far_ref, sib_far_ref)

    @pl.when(odd == 1)
    def _():
        both(sib_cuts_ref, cuts_ref, sib_ref, features_ref, sib_far_ref, far_ref)


def agg_kernel(cuts_ref, features_ref, near_ref, far_ref, out_ref):
    values = features_ref[...].astype(jnp.float32)
    link = links(cuts_ref, *values.shape)
    odd = lax.rem(lax.axis_index("col"), 2) == 1
    near = near_ref[...].astype(jnp.float32)
    far = far_ref[...].astype(jnp.float32)
    prev = jnp.where(odd, near[15:16], far[15:16])
    nxt = jnp.where(odd, far[0:1], near[0:1])
    out_ref[...] = stencil(values, link, prev, nxt).astype(out_ref.dtype)


class Slots:
    def __init__(self, slots, negatives, cut_count):
        self.slots, self.negatives = slots, negatives
        self.rows, self.cols, self.keys = 0, slots, 2 * slots
        self.nrows = 3 * slots
        self.ncols = self.nrows + negatives
        self.count = self.ncols + negatives
        self.cuts = self.count + 1
        self.cut_count = cut_count
        self.end = self.cuts + cut_count


def count_kernel(at, base, blocks, cols, per, meta_ref, n_ref):
    here_rows = per * 2 * (lax.axis_index("col") // 2)
    here_cols = per * lax.axis_index("row")
    width = cols * BLOCK
    total = jnp.zeros((blocks, width), jnp.float32)
    count = meta_ref[0:1, at.count : at.count + 1]
    for rows_at, cols_at, slots, positive in (
        (at.rows, at.cols, at.slots, True),
        (at.nrows, at.ncols, at.negatives, False),
    ):
        rows = jnp.bitwise_xor(meta_ref[0:1, rows_at : rows_at + slots], here_rows) - base
        cols_of = jnp.bitwise_xor(meta_ref[0:1, cols_at : cols_at + slots], here_cols)
        hit = lax.broadcasted_iota(jnp.int32, (blocks, slots), 0) == rows
        if positive:
            live = lax.broadcasted_iota(jnp.int32, (blocks, slots), 1) < count
            hit = jnp.logical_and(hit, live)
        lane = lax.shift_right_logical(lax.broadcasted_iota(jnp.int32, (width, slots), 0), 7)
        spread = jnp.where(lane == cols_of, 1.0, 0.0).astype(jnp.bfloat16)
        total += lax.dot_general(
            jnp.where(hit, 0.5, 0.0).astype(jnp.bfloat16), spread,
            (((1,), (1,)), ((), ())), preferred_element_type=jnp.float32,
        )
    n_ref[...] = total


def counts(at, base, blocks, cols, per, meta):
    return pl.pallas_call(
        functools.partial(count_kernel, at, base, blocks, cols, per),
        out_shape=jax.ShapeDtypeStruct((blocks, cols * BLOCK), jnp.float32),
        in_specs=[VMEM],
        out_specs=VMEM,
        compiler_params=params(8),
    )(meta)


def target_kernel(at, base, blocks, cols, per, part, parts, filtered, meta_s, *refs):
    t_ref, step_ref = refs[-2:]
    a = lax.broadcasted_iota(jnp.int32, (BLOCK, BLOCK), 0)
    b = lax.broadcasted_iota(jnp.int32, (BLOCK, BLOCK), 1)
    step_ref[...] = (a * BLOCK + b) * jnp.int32(4 * 40503)
    if part == 0:

        def clear(i, _):
            row = pl.multiple_of(i * BLOCK, BLOCK)
            t_ref[pl.ds(row, BLOCK), :] = jnp.zeros((BLOCK, cols * BLOCK), jnp.float32)
            return 0

        lax.fori_loop(0, blocks, clear, 0)
    here_rows = per * 2 * (lax.axis_index("col") // 2)
    here_cols = per * lax.axis_index("row")
    count = meta_s[0, at.count]
    unroll = 8 if at.slots % 8 == 0 else 1

    def positive(s):
        i = jnp.bitwise_xor(meta_s[0, at.rows + s], here_rows) - base
        j = jnp.bitwise_xor(meta_s[0, at.cols + s], here_cols)
        key = meta_s[0, at.keys + s] * 4
        one = jnp.where(s < count, 1.0, 0.0).astype(jnp.float32)

        def add():
            row = pl.multiple_of(i * BLOCK, BLOCK)
            col = pl.multiple_of(j * BLOCK, BLOCK)
            mixed = step_ref[...] + key
            mixed = jnp.bitwise_xor(mixed, lax.shift_right_logical(mixed, 11))
            fifth = lax.shift_right_logical(mixed, 9) * jnp.int32(INV5)
            hit = fifth.astype(jnp.uint32) < jnp.uint32(2**21)
            t_ref[pl.ds(row, BLOCK), pl.ds(col, BLOCK)] += jnp.where(hit, one, 0.0)

        if filtered:
            pl.when(jnp.logical_and(i >= 0, i < blocks))(add)
        else:
            add()

    def positives(g, _):
        for u in range(unroll):
            positive(g * unroll + u)
        return 0

    trips = (count + unroll - 1) // unroll
    lax.fori_loop(trips * part // parts, trips * (part + 1) // parts, positives, 0)


def targets(at, base, blocks, cols, per, part, parts, filtered, meta, before):
    shape = (blocks * BLOCK, cols * BLOCK)
    old = [] if before is None else [before]
    return pl.pallas_call(
        functools.partial(target_kernel, at, base, blocks, cols, per, part, parts, filtered),
        out_shape=jax.ShapeDtypeStruct(shape, jnp.float32),
        in_specs=[SMEM] + [VMEM] * len(old),
        out_specs=VMEM,
        input_output_aliases={1: 0} if old else {},
        scratch_shapes=[pltpu.VMEM((BLOCK, BLOCK), jnp.int32)],
        compiler_params=params(10),
        cost_estimate=pl.CostEstimate(
            flops=at.slots * BLOCK * BLOCK * 10 // parts,
            bytes_accessed=at.slots * BLOCK * BLOCK * 8 // parts,
            transcendentals=0,
        ),
    )(meta, *old)


def decode_kernel(nz, nrow, first, count, refs):
    steps = max(nz, nrow) - 1
    t_ref, n_ref, weight_ref, pair_ref = refs[:4]
    recv = refs[4 : 4 + steps]
    other = refs[4 + steps : 4 + 2 * steps]
    refs = refs[4 + 2 * steps :]
    keep_ref, give_ref = refs[:2]
    messages = refs[2 : 2 + nrow]
    row_agg, col_agg, row_z, col_z, col_acc = refs[2 + nrow :]
    shard = pair_ref.shape[0] // 2
    per = shard // BLOCK
    core = lax.rem(lax.axis_index("col"), 2)

    def gather(z_refs, row_refs, side):
        for k in range(count):
            ref = pair_ref if first + k == 0 else z_refs[first + k - 1]
            row_agg[2 * k * shard : 2 * (k + 1) * shard, :] = ref[...]
        for q in range(nrow):
            ref = pair_ref if q == 0 else row_refs[q - 1]
            col_agg[q * shard : (q + 1) * shard, :] = ref[side * shard : (side + 1) * shard, :]

    pl.when(core == 0)(lambda: gather(recv, other, 0))
    pl.when(core == 1)(lambda: gather(other, recv, 1))

    weight = weight_ref[...]
    dots = functools.partial(lax.dot_general, preferred_element_type=jnp.float32)
    nn = (((1,), (0,)), ((), ()))
    nt = (((1,), (1,)), ((), ()))
    tn = (((0,), (0,)), ((), ()))
    for q in range(nrow):
        at = slice(q * shard, (q + 1) * shard)
        col_z[at, :] = dots(col_agg[at, :], weight, nn).astype(jnp.bfloat16)
    for p in range(2 * count):
        at = slice(p * shard, (p + 1) * shard)
        row_z[at, :] = dots(row_agg[at, :], weight, nn).astype(jnp.bfloat16)
    share = jnp.zeros(weight.shape, jnp.float32)
    for k in range(count):
        drows = []
        for p in (2 * k, 2 * k + 1):
            near = row_z[p * shard : (p + 1) * shard, :]
            half = near * jnp.bfloat16(0.5)
            drow = None
            for q in range(nrow):
                far = col_z[q * shard : (q + 1) * shard, :]
                curve = jnp.tanh(dots(half, far, nt))
                bands = []
                for i in range(per):
                    band = slice(i * BLOCK, (i + 1) * BLOCK)
                    n = n_ref[p * per + i : p * per + i + 1, q * shard : (q + 1) * shard]
                    row = p * shard + i * BLOCK
                    tile = t_ref[row : row + BLOCK, q * shard : (q + 1) * shard]
                    bands.append((n * curve[band] + (n - tile)).astype(jnp.bfloat16))
                grad = jnp.concatenate(bands, axis=0)
                term = dots(grad, far, nn)
                drow = term if drow is None else drow + term
                back = dots(grad, near, tn)
                if p == 0:
                    col_acc[q * shard : (q + 1) * shard, :] = back
                else:
                    col_acc[q * shard : (q + 1) * shard, :] += back
            drow = drow * (1.0 / 32.0)
            share += dots(row_agg[p * shard : (p + 1) * shard, :], drow.astype(jnp.bfloat16), tn)
            drows.append(drow)
        at = slice(k * shard, (k + 1) * shard)
        keep_ref[at, :] = jnp.where(core == 0, drows[0], drows[1])
        give_ref[at, :] = jnp.where(core == 0, drows[1], drows[0]).astype(give_ref.dtype)
    for q in range(nrow):
        at = slice(q * shard, (q + 1) * shard)
        rounded = (col_acc[at, :] * (1.0 / 32.0)).astype(jnp.bfloat16)
        messages[q][0:shard, :] = rounded
        share += dots(col_agg[at, :], rounded, tn)
    for q in range(nrow):
        messages[q][shard:, :] = share.astype(messages[q].dtype)


def decode(t, n, weight, pair, recv, other, nz, nrow, first, count):
    shard = pair.shape[0] // 2
    width = weight.shape[1]
    bf16, real = jnp.bfloat16, jnp.float32
    outs = [
        jax.ShapeDtypeStruct((count * shard, width), real),
        jax.ShapeDtypeStruct((count * shard, width), bf16),
    ]
    outs += [jax.ShapeDtypeStruct((shard + weight.shape[0], width), bf16)] * nrow
    result = pl.pallas_call(
        lambda *refs: decode_kernel(nz, nrow, first, count, refs),
        out_shape=outs,
        in_specs=[VMEM] * (4 + len(recv) + len(other)),
        out_specs=[VMEM] * len(outs),
        scratch_shapes=[
            pltpu.VMEM((2 * count * shard, width), bf16),
            pltpu.VMEM((nrow * shard, width), bf16),
            pltpu.VMEM((2 * count * shard, width), bf16),
            pltpu.VMEM((nrow * shard, width), bf16),
            pltpu.VMEM((nrow * shard, width), real),
        ],
        compiler_params=params(24),
        cost_estimate=pl.CostEstimate(
            flops=6 * t.shape[0] * t.shape[1] * width,
            bytes_accessed=t.shape[0] * t.shape[1] * 2,
            transcendentals=t.shape[0] * t.shape[1],
        ),
    )(t, n, weight, pair, *recv, *other)
    return result[0], result[1], result[2:]


def latent_kernel(nz, nrow, cuts_ref, weight_ref, *refs):
    shard = refs[0].shape[0]
    dagg_ref, edge_ref = refs[nz + nrow :]
    total = refs[0][...].astype(jnp.float32)
    for part in refs[1:nz]:
        total += part[...].astype(jnp.float32)
    for part in refs[nz : nz + nrow]:
        total += part[0:shard, :].astype(jnp.float32)
    dlatent = total.astype(jnp.bfloat16)
    dagg = lax.dot_general(
        dlatent, weight_ref[...], (((1,), (1,)), ((), ())), preferred_element_type=jnp.float32
    ).astype(jnp.bfloat16)
    dagg_ref[...] = dagg
    values = dagg.astype(jnp.float32)
    edges(values, links(cuts_ref, *values.shape), edge_ref)


def f32(x):
    return x.astype(jnp.float32)


def tree_sum(parts):
    parts = [f32(x) for x in parts]
    while len(parts) > 1:
        parts = [a + b for a, b in zip(parts[::2], parts[1::2])]
    return parts[0]


def local(features, weight, cuts, pos_rows, pos_cols, pos_keys, pos_count, neg_rows, neg_cols):
    shard, width = features.shape
    ncol = lax.axis_size("col")
    nrow = lax.axis_size("row")
    nz = ncol // 2
    per = shard // BLOCK
    steps = max(nz, nrow)
    bf16 = jnp.bfloat16
    message = jax.ShapeDtypeStruct((16, width), bf16)
    sib, sib_cuts = swap(features, "col", 1), swap(cuts, "col", 1)
    ends = pl.pallas_call(
        edge_kernel, out_shape=message, in_specs=[SMEM, VMEM], out_specs=VMEM,
        compiler_params=params(2),
    )(cuts, features)
    far = swap_next(ends)
    cols = nrow * per
    pieces = max(1, ncol * per * cols // CHUNK_CELLS)
    blocks = ncol * per // pieces
    parts = PARTS if pieces == 1 else 1
    slots = [x.reshape(1, -1) for x in (pos_rows, pos_cols, pos_keys, neg_rows, neg_cols, pos_count)]
    at = Slots(slots[0].shape[1], slots[3].shape[1], 0)
    meta = jnp.concatenate(slots + [jnp.zeros((1, -at.end % BLOCK), jnp.int32)], axis=1)
    found = [
        targets(at, k * blocks, blocks, cols, per, 0, parts, pieces > 1, meta, None)
        for k in range(pieces)
    ]
    number = [counts(at, k * blocks, blocks, cols, per, meta) for k in range(pieces)]
    if pieces == 1:
        far, found = lax.optimization_barrier((far, found))
    sib_far = swap(far, "col", 1)
    pair = pl.pallas_call(
        pair_kernel,
        out_shape=jax.ShapeDtypeStruct((2 * shard, width), bf16),
        in_specs=[SMEM, SMEM] + [VMEM] * 4,
        out_specs=VMEM,
        compiler_params=params(4),
    )(cuts, sib_cuts, features, sib, far, sib_far)
    recv = [swap_mixed(pair, k) for k in range(1, steps)]
    if pieces == 1:
        t = targets(at, 0, blocks, cols, per, 1, parts, False, meta, found[0])
        recv, t = lax.optimization_barrier((recv, t))
        other = [swap(x, "col", 1) for x in recv]
        t = targets(at, 0, blocks, cols, per, 2, parts, False, meta, t)
        found = [t]
    else:
        other = [swap(x, "col", 1) for x in recv]
    count = nz // pieces
    keeps, gives, messages = [], [], []
    for k, (t, n) in enumerate(zip(found, number)):
        out = decode(t, n, weight, pair, recv, other, nz, nrow, k * count, count)
        keeps.append(out[0])
        gives.append(out[1])
        messages.append(out[2])
    messages = messages[0] if pieces == 1 else [tree_sum(x).astype(bf16) for x in zip(*messages)]
    give = gives[0] if pieces == 1 else jnp.concatenate(gives, axis=0)
    keep = keeps[0] if pieces == 1 else jnp.concatenate(keeps, axis=0)
    got = swap(give, "col", 1)
    columns = [messages[0]] + [swap(messages[k], "row", k) for k in range(1, nrow)]
    kept = [
        (keep[k * shard : (k + 1) * shard] + f32(got[k * shard : (k + 1) * shard])).astype(bf16)
        for k in range(nz)
    ]
    rows = [kept[0]] + [swap(kept[k], "col", 2 * k) for k in range(1, nz)]
    share = tree_sum([x[shard:] for x in columns])
    share = (share + swap(share, "col", 1)).astype(bf16)
    dagg, dends = pl.pallas_call(
        functools.partial(latent_kernel, nz, nrow),
        out_shape=(jax.ShapeDtypeStruct(features.shape, bf16), message),
        in_specs=[SMEM, VMEM] + [VMEM] * (nz + nrow),
        out_specs=(VMEM, VMEM),
        compiler_params=params(6),
    )(cuts, weight, *rows, *columns)
    near, far = swap(dends, "col", 1), swap_next(dends)
    share = tree_sum([share] + [swap(share, "col", 2 * k) for k in range(1, nz)])
    grad_features = pl.pallas_call(
        agg_kernel,
        out_shape=jax.ShapeDtypeStruct(features.shape, bf16),
        in_specs=[SMEM, VMEM, VMEM, VMEM],
        out_specs=VMEM,
        compiler_params=params(4),
    )(cuts, dagg, near, far)
    grad_weight = share * (shard * ncol * nrow) ** (-0.5)
    return (grad_features, grad_weight)


def solution(mesh):
    placed = (
        P(AXES, None),
        P(),
        P(AXES, None),
        P("row", "col", None),
        P("row", "col", None),
        P("row", "col", None),
        P("row", "col"),
        P("row", "col", None),
        P("row", "col", None),
    )
    return jax.shard_map(
        local, mesh=mesh, in_specs=placed, out_specs=(P(AXES, None), P()), check_vma=False
    )
```

```python
import functools

import jax
import jax.numpy as jnp
from jax import lax
from jax.experimental import pallas as pl
from jax.experimental.pallas import tpu as pltpu
from jax.sharding import PartitionSpec as P

BLOCK = 128
AXES = ("row", "col")
INV5 = -858993459
VMEM = pl.BlockSpec(memory_space=pltpu.VMEM)
SMEM = pl.BlockSpec(memory_space=pltpu.SMEM)
CHUNK_CELLS = 128
BOUNDS = (0, 11, 52, 64)


def params(mib):
    return pltpu.CompilerParams(vmem_limit_bytes=mib * 2**20)


def swap(x, axis, step):
    count = lax.axis_size(axis)
    return lax.ppermute(x, axis, [(i, i ^ step) for i in range(count)])


def swap_next(x):
    count = lax.axis_size("row") * lax.axis_size("col")
    pairs = [(0, 0), (count - 1, count - 1)]
    for s in range(1, count - 1, 2):
        pairs += [(s, s + 1), (s + 1, s)]
    return lax.ppermute(x, AXES, pairs)


def inner(axis_end):
    chips = lax.axis_size("row") * lax.axis_size("col") // 2
    chip = (lax.axis_index("row") * lax.axis_size("col") + lax.axis_index("col")) // 2
    return jnp.where(chip == (chips - 1 if axis_end else 0), 0.0, 1.0).astype(jnp.float32)


def swap_mixed(x, step):
    nrow, ncol = lax.axis_size("row"), lax.axis_size("col")
    pairs = []
    for r in range(nrow):
        for c in range(ncol):
            if c % 2 == 0 and step < ncol // 2:
                pairs.append((r * ncol + c, r * ncol + (c ^ (2 * step))))
            if c % 2 == 1 and step < nrow:
                pairs.append((r * ncol + c, (r ^ step) * ncol + c))
    return lax.ppermute(x, AXES, pairs)


def edges(values, link, out_ref):
    rows, width = values.shape
    head = link[0:8] * values[0:8]
    tail = values[rows - 8 : rows]
    out_ref[...] = jnp.concatenate([head, tail], axis=0).astype(out_ref.dtype)


def stencil(values, link, prev, nxt):
    rows, width = values.shape
    node = lax.broadcasted_iota(jnp.int32, (rows, width), 0)
    before = jnp.where(node == 0, prev, pltpu.roll(values, 1, 0))
    after = jnp.where(node == rows - 1, nxt, pltpu.roll(link * values, rows - 1, 0))
    return 0.5 * values + 0.25 * (link * before + after)


def parity(even, odd):
    side = lax.rem(lax.axis_index("col"), 2)
    pl.when(side == 0)(even)
    pl.when(side == 1)(odd)


def body_kernel(at, features_hbm, rows, cols, keys, nrows, ncols, cuts_hbm, count_s, *refs):
    body_ref, ends_ref, meta_ref, cuts_s, sems = refs
    shard, width = features_hbm.shape
    pairs = [(cuts_hbm, cuts_s), (features_hbm, body_ref.at[pl.ds(0, shard), :])]
    for source, spot in (
        (rows, at.rows), (cols, at.cols), (keys, at.keys), (nrows, at.nrows), (ncols, at.ncols),
    ):
        pairs.append((source.at[0], meta_ref.at[:, pl.ds(spot, source.shape[2])]))
    copies = [pltpu.make_async_copy(a, b, sems.at[t]) for t, (a, b) in enumerate(pairs)]
    for copy in copies:
        copy.start()
    meta_ref[:, at.count :] = jnp.full((1, meta_ref.shape[1] - at.count), count_s[0, 0], jnp.int32)
    node = lax.broadcasted_iota(jnp.int32, (shard, width), 0)
    copies[0].wait()
    cut = node == cuts_s[0, 0]
    for t in range(1, cuts_s.shape[1]):
        cut = jnp.logical_or(cut, node == cuts_s[0, t])
    link = jnp.where(cut, 0.0, 1.0).astype(jnp.float32)
    body_ref[shard:, :] = link.astype(body_ref.dtype)
    for copy in copies[1:]:
        copy.wait()
    edges(body_ref[0:shard, :].astype(jnp.float32), link, ends_ref)


def bodies(at, features, slots, cuts, count):
    shard, width = features.shape
    pinned = [pltpu.with_memory_space_constraint(x, pltpu.HBM) for x in (features, *slots, cuts)]
    hbm = pl.BlockSpec(memory_space=pltpu.HBM)
    return pl.pallas_call(
        functools.partial(body_kernel, at),
        out_shape=(
            jax.ShapeDtypeStruct((2 * shard, width), features.dtype),
            jax.ShapeDtypeStruct((16, width), features.dtype),
            jax.ShapeDtypeStruct((1, at.end), jnp.int32),
        ),
        in_specs=[hbm] * len(pinned) + [SMEM],
        out_specs=(VMEM, VMEM, VMEM),
        scratch_shapes=[
            pltpu.SMEM(cuts.shape, jnp.int32),
            pltpu.SemaphoreType.DMA((len(pinned),)),
        ],
        compiler_params=params(4),
    )(*pinned, count)


def pair_kernel(body_ref, sib_ref, far_ref, sib_far_ref, out_ref):
    shard = body_ref.shape[0] // 2

    def both(first_ref, second_ref, before_ref, after_ref):
        first = first_ref[0:shard, :].astype(jnp.float32)
        second = second_ref[0:shard, :].astype(jnp.float32)
        first_link = first_ref[shard:, :].astype(jnp.float32)
        second_link = second_ref[shard:, :].astype(jnp.float32)
        prev = before_ref[...].astype(jnp.float32)[15:16] * inner(False)
        nxt = after_ref[...].astype(jnp.float32)[0:1] * inner(True)
        head = second_link[0:1] * second[0:1]
        tail = first[shard - 1 : shard]
        out_ref[0:shard, :] = stencil(first, first_link, prev, head).astype(out_ref.dtype)
        out_ref[shard:, :] = stencil(second, second_link, tail, nxt).astype(out_ref.dtype)

    parity(
        lambda: both(body_ref, sib_ref, far_ref, sib_far_ref),
        lambda: both(sib_ref, body_ref, sib_far_ref, far_ref),
    )


class Slots:
    def __init__(self, slots, negatives):
        self.slots, self.negatives = slots, negatives
        self.rows, self.cols, self.keys = 0, slots, 2 * slots
        self.nrows = 3 * slots
        self.ncols = self.nrows + negatives
        self.count = self.ncols + negatives
        self.end = self.count + BLOCK


def count_kernel(at, base, blocks, cols, per, meta_ref, n_ref):
    here_rows = per * 2 * (lax.axis_index("col") // 2)
    here_cols = per * lax.axis_index("row")
    width = cols * BLOCK
    total = jnp.zeros((blocks, width), jnp.float32)
    count = meta_ref[0:1, at.count : at.count + 1]
    for rows_at, cols_at, slots, positive in (
        (at.rows, at.cols, at.slots, True),
        (at.nrows, at.ncols, at.negatives, False),
    ):
        rows = jnp.bitwise_xor(meta_ref[0:1, rows_at : rows_at + slots], here_rows) - base
        cols_of = jnp.bitwise_xor(meta_ref[0:1, cols_at : cols_at + slots], here_cols)
        hit = lax.broadcasted_iota(jnp.int32, (blocks, slots), 0) == rows
        if positive:
            live = lax.broadcasted_iota(jnp.int32, (blocks, slots), 1) < count
            hit = jnp.logical_and(hit, live)
        lane = lax.shift_right_logical(lax.broadcasted_iota(jnp.int32, (width, slots), 0), 7)
        spread = jnp.where(lane == cols_of, 1.0, 0.0).astype(jnp.bfloat16)
        total += lax.dot_general(
            jnp.where(hit, 0.5, 0.0).astype(jnp.bfloat16), spread,
            (((1,), (1,)), ((), ())), preferred_element_type=jnp.float32,
        )
    n_ref[...] = total


def counts(at, base, blocks, cols, per, meta):
    return pl.pallas_call(
        functools.partial(count_kernel, at, base, blocks, cols, per),
        out_shape=jax.ShapeDtypeStruct((blocks, cols * BLOCK), jnp.float32),
        in_specs=[VMEM],
        out_specs=VMEM,
        compiler_params=params(8),
    )(meta)


def target_kernel(at, base, blocks, cols, per, part, bounds, filtered, meta_s, *refs):
    t_ref, step_ref = refs[-2:]
    a = lax.broadcasted_iota(jnp.int32, (BLOCK, BLOCK), 0)
    b = lax.broadcasted_iota(jnp.int32, (BLOCK, BLOCK), 1)
    step_ref[...] = (a * BLOCK + b) * jnp.int32(4 * 40503)
    if part == 0:

        def clear(i, _):
            row = pl.multiple_of(i * BLOCK, BLOCK)
            t_ref[pl.ds(row, BLOCK), :] = jnp.zeros((BLOCK, cols * BLOCK), jnp.float32)
            return 0

        lax.fori_loop(0, blocks, clear, 0)
    here_rows = per * 2 * (lax.axis_index("col") // 2)
    here_cols = per * lax.axis_index("row")
    count = meta_s[0, at.count]
    unroll = 8 if at.slots % 8 == 0 else 1

    def positive(s):
        i = jnp.bitwise_xor(meta_s[0, at.rows + s], here_rows) - base
        j = jnp.bitwise_xor(meta_s[0, at.cols + s], here_cols)
        key = meta_s[0, at.keys + s] * 4
        one = jnp.where(s < count, 1.0, 0.0).astype(jnp.float32)

        def add():
            row = pl.multiple_of(i * BLOCK, BLOCK)
            col = pl.multiple_of(j * BLOCK, BLOCK)
            mixed = step_ref[...] + key
            mixed = jnp.bitwise_xor(mixed, lax.shift_right_logical(mixed, 11))
            fifth = lax.shift_right_logical(mixed, 9) * jnp.int32(INV5)
            hit = fifth.astype(jnp.uint32) < jnp.uint32(2**21)
            t_ref[pl.ds(row, BLOCK), pl.ds(col, BLOCK)] += jnp.where(hit, one, 0.0)

        if filtered:
            pl.when(jnp.logical_and(i >= 0, i < blocks))(add)
        else:
            add()

    def positives(g, _):
        for u in range(unroll):
            positive(g * unroll + u)
        return 0

    trips = (count + unroll - 1) // unroll
    first, last = bounds[part], bounds[part + 1]
    lax.fori_loop(trips * first // 64, trips * last // 64, positives, 0)


def targets(at, base, blocks, cols, per, part, bounds, filtered, meta, before):
    shape = (blocks * BLOCK, cols * BLOCK)
    old = [] if before is None else [before]
    return pl.pallas_call(
        functools.partial(target_kernel, at, base, blocks, cols, per, part, bounds, filtered),
        out_shape=jax.ShapeDtypeStruct(shape, jnp.float32),
        in_specs=[SMEM] + [VMEM] * len(old),
        out_specs=VMEM,
        input_output_aliases={1: 0} if old else {},
        scratch_shapes=[pltpu.VMEM((BLOCK, BLOCK), jnp.int32)],
        compiler_params=params(10),
        cost_estimate=pl.CostEstimate(
            flops=at.slots * BLOCK * BLOCK * 4,
            bytes_accessed=at.slots * BLOCK * BLOCK * 4,
            transcendentals=0,
        ),
    )(meta, *old)


def decode_kernel(nz, nrow, first, count, refs):
    steps = max(nz, nrow) - 1
    t_ref, n_ref, weight_ref, pair_ref = refs[:4]
    recv = refs[4 : 4 + steps]
    other = refs[4 + steps : 4 + 2 * steps]
    refs = refs[4 + 2 * steps :]
    drow_ref, give_ref, grad_ref, row_agg, col_agg, row_z = refs[:6]
    (col_z,) = refs[6:]
    pair = pair_ref.shape[0]
    shard = pair // 2
    columns = nrow * shard
    bf16 = jnp.bfloat16

    def gather(z_refs, row_refs, side):
        for k in range(count):
            ref = pair_ref if first + k == 0 else z_refs[first + k - 1]
            row_agg[k * pair : (k + 1) * pair, :] = ref[...]
        for q in range(nrow):
            ref = pair_ref if q == 0 else row_refs[q - 1]
            col_agg[q * shard : (q + 1) * shard, :] = ref[side * shard : (side + 1) * shard, :]

    parity(lambda: gather(recv, other, 0), lambda: gather(other, recv, 1))
    weight = weight_ref[...]
    dots = functools.partial(lax.dot_general, preferred_element_type=jnp.float32)
    nn = (((1,), (0,)), ((), ()))
    nt = (((1,), (1,)), ((), ()))
    tn = (((0,), (0,)), ((), ()))
    col_z[...] = dots(col_agg[...], weight, nn).astype(bf16)
    for k in range(count):
        at = slice(k * pair, (k + 1) * pair)
        row_z[at, :] = dots(row_agg[at, :], weight, nn).astype(bf16)
        half = row_z[at, :] * bf16(0.5)
        for c in range(0, columns, pair):
            cut = slice(c, min(c + pair, columns))
            curve = jnp.tanh(dots(half, col_z[cut, :], nt))
            for i in range(pair // BLOCK):
                row = k * pair + i * BLOCK
                n = n_ref[row // BLOCK : row // BLOCK + 1, cut]
                tile = t_ref[row : row + BLOCK, cut]
                part = n * curve[i * BLOCK : (i + 1) * BLOCK] + (n - tile)
                grad_ref[row : row + BLOCK, cut] = part.astype(bf16)
        drow = dots(grad_ref[at, :], col_z[...], nn) * (1.0 / 32.0)
        drow_ref[at, :] = drow
        give_ref[at, :] = drow.astype(bf16)


def column_kernel(grad_ref, row_agg, col_agg, row_z, drow_ref, dcol_ref, give_ref, share_ref):
    dots = functools.partial(lax.dot_general, preferred_element_type=jnp.float32)
    nn = (((1,), (0,)), ((), ()))
    tn = (((0,), (0,)), ((), ()))
    bf16 = jnp.bfloat16
    columns = dcol_ref.shape[0]
    row_t = row_z[...].T
    step = min(columns, 4 * BLOCK)
    for c in range(0, columns, step):
        cut = slice(c, c + step)
        dcol = dots(row_t, grad_ref[:, cut], nn).T * (1.0 / 32.0)
        dcol_ref[cut, :] = dcol
        give_ref[cut, :] = dcol.astype(bf16)
    share = dots(row_agg[...], drow_ref[...].astype(bf16), tn)
    share += dots(col_agg[...], give_ref[0:columns, :], tn)
    share_ref[...] = share
    give_ref[columns:, :] = share.astype(bf16)


def decode(t, n, weight, pair, recv, other, nz, nrow, first, count):
    rows, columns = t.shape
    width = weight.shape[1]
    bf16, real = jnp.bfloat16, jnp.float32
    shape = jax.ShapeDtypeStruct
    outs = [
        shape((rows, width), real),
        shape((rows, width), bf16),
        shape((rows, columns), bf16),
        shape((rows, width), bf16),
        shape((columns, width), bf16),
        shape((rows, width), bf16),
    ]
    drow, give_rows, grad, row_agg, col_agg, row_z = pl.pallas_call(
        lambda *refs: decode_kernel(nz, nrow, first, count, refs),
        out_shape=outs,
        in_specs=[VMEM] * (4 + len(recv) + len(other)),
        out_specs=[VMEM] * len(outs),
        scratch_shapes=[pltpu.VMEM((columns, width), bf16)],
        compiler_params=params(12),
        cost_estimate=pl.CostEstimate(
            flops=4 * rows * columns * width,
            bytes_accessed=rows * columns * 4,
            transcendentals=rows * columns,
        ),
    )(t, n, weight, pair, *recv, *other)
    dcol, give_columns, share = call(
        column_kernel,
        (
            shape((columns, width), real),
            shape((columns + weight.shape[0], width), bf16),
            shape(weight.shape, real),
        ),
        (grad, row_agg, col_agg, row_z, drow), 10,
    )
    return drow, give_rows, dcol, give_columns, share


def merge_kernel(nz, nrow, drow_ref, dcol_ref, share_ref, rows_ref, columns_ref, *messages):
    messages, chip_ref = messages[:-1], messages[-1]
    width = share_ref.shape[0]
    pair = messages[0].shape[0]
    shard = pair // 2
    bf16 = jnp.bfloat16

    def rows():
        for k in range(nz):
            at = slice(k * pair, (k + 1) * pair)
            total = drow_ref[at, :] + rows_ref[at, :].astype(jnp.float32)
            messages[k][...] = total.astype(bf16)

    def columns():
        for q in range(nrow):
            at = slice(q * shard, (q + 1) * shard)
            messages[q][0:shard, :] = columns_ref[at, :]
            messages[q][shard:pair, :] = dcol_ref[at, :].astype(bf16)

    parity(rows, columns)
    share = columns_ref[columns_ref.shape[0] - width :, :].astype(jnp.float32)
    chip_ref[...] = (share_ref[...].astype(bf16).astype(jnp.float32) + share).astype(bf16)


def tree_sum(parts):
    parts = [x.astype(jnp.float32) for x in parts]
    while len(parts) > 1:
        parts = [a + b for a, b in zip(parts[::2], parts[1::2])]
    return parts[0]


def sum_kernel(*refs):
    refs[-1][...] = tree_sum([x[...] for x in refs[:-1]]).astype(refs[-1].dtype)


def latent_kernel(mine_ref, theirs_ref, weight_ref, body_ref, dagg_ref, ends_ref):
    shard = mine_ref.shape[0] // 2
    dlatent = (mine_ref[...] + theirs_ref[...]).astype(jnp.bfloat16)
    dagg = lax.dot_general(
        dlatent, weight_ref[...], (((1,), (1,)), ((), ())), preferred_element_type=jnp.float32
    ).astype(jnp.bfloat16)
    dagg_ref[...] = dagg
    link = body_ref[shard:, :].astype(jnp.float32)

    def side(which):
        values = dagg[which * shard : (which + 1) * shard].astype(jnp.float32)
        edges(values, link, ends_ref)

    parity(lambda: side(0), lambda: side(1))


def final_kernel(scale, dagg_ref, body_ref, sib_ref, far_ref, *refs):
    shares, (features_ref, weight_ref) = refs[:-2], refs[-2:]
    shard = features_ref.shape[0]
    link = body_ref[shard:, :].astype(jnp.float32)

    def even():
        values = dagg_ref[0:shard, :].astype(jnp.float32)
        prev = far_ref[...].astype(jnp.float32)[15:16] * inner(False)
        nxt = sib_ref[shard : shard + 8, :].astype(jnp.float32)[0:1]
        nxt = nxt * dagg_ref[shard : shard + 8, :].astype(jnp.float32)[0:1]
        features_ref[...] = stencil(values, link, prev, nxt).astype(features_ref.dtype)

    def odd():
        values = dagg_ref[shard:, :].astype(jnp.float32)
        prev = dagg_ref[shard - 8 : shard, :].astype(jnp.float32)[7:8]
        nxt = far_ref[...].astype(jnp.float32)[0:1] * inner(True)
        features_ref[...] = stencil(values, link, prev, nxt).astype(features_ref.dtype)

    parity(even, odd)
    weight_ref[...] = tree_sum([x[...] for x in shares]) * scale


def call(kernel, outs, operands, mib, specs=None):
    return pl.pallas_call(
        kernel,
        out_shape=outs,
        in_specs=specs or [VMEM] * len(operands),
        out_specs=jax.tree.map(lambda _: VMEM, outs),
        compiler_params=params(mib),
    )(*operands)


def local(features, weight, cuts, pos_rows, pos_cols, pos_keys, pos_count, neg_rows, neg_cols):
    shard, width = features.shape
    ncol = lax.axis_size("col")
    nrow = lax.axis_size("row")
    nz = ncol // 2
    per = shard // BLOCK
    steps = max(nz, nrow)
    bf16, real = jnp.bfloat16, jnp.float32
    shape = jax.ShapeDtypeStruct
    message = shape((16, width), bf16)

    at = Slots(pos_rows.shape[2], neg_rows.shape[2])
    slots = (pos_rows, pos_cols, pos_keys, neg_rows, neg_cols)
    body, ends, meta = bodies(at, features, slots, cuts, pos_count)
    far = swap_next(ends)
    sib = swap(body, "col", 1)
    cols = nrow * per
    pieces = max(1, ncol * per * cols // CHUNK_CELLS)
    blocks = ncol * per // pieces
    bounds = BOUNDS if pieces == 1 else (0, 64)
    found = [
        targets(at, k * blocks, blocks, cols, per, 0, bounds, pieces > 1, meta, None)
        for k in range(pieces)
    ]
    number = [counts(at, k * blocks, blocks, cols, per, meta) for k in range(pieces)]
    if pieces == 1:
        far, found, number = lax.optimization_barrier((far, found, number))
    sib_far = swap(far, "col", 1)
    pair = call(pair_kernel, shape((2 * shard, width), bf16), (body, sib, far, sib_far), 4)
    recv = [swap_mixed(pair, k) for k in range(steps - 1, 0, -1)][::-1]
    if pieces == 1:
        t = targets(at, 0, blocks, cols, per, 1, bounds, False, meta, found[0])
        recv, t = lax.optimization_barrier((recv, t))
        other = [swap(x, "col", 1) for x in recv]
        found = [targets(at, 0, blocks, cols, per, 2, bounds, False, meta, t)]
    else:
        other = [swap(x, "col", 1) for x in recv]
    count = nz // pieces
    outs = [
        decode(t, n, weight, pair, recv, other, nz, nrow, k * count, count)
        for k, (t, n) in enumerate(zip(found, number))
    ]
    if pieces == 1:
        drow, give_rows, dcol, give_columns, share = outs[0]
    else:
        drow = jnp.concatenate([x[0] for x in outs], axis=0)
        give_rows = jnp.concatenate([x[1] for x in outs], axis=0)
        dcol, share = (tree_sum([x[k] for x in outs]) for k in (2, 4))
        give_columns = jnp.concatenate([dcol, share], axis=0).astype(bf16)
    got_rows, got_columns = swap(give_rows, "col", 1), swap(give_columns, "col", 1)
    *messages, share = call(
        functools.partial(merge_kernel, nz, nrow),
        [shape((2 * shard, width), bf16)] * steps + [shape(weight.shape, bf16)],
        (drow, dcol, share, got_rows, got_columns), 8,
    )
    arrived = [swap_mixed(messages[k], k) for k in range(steps - 1, 0, -1)]
    arrived = [messages[0]] + arrived[::-1]
    shares = [share] + [swap(share, "row", k) for k in range(1, nrow)]
    share = call(sum_kernel, shape(weight.shape, bf16), shares, 4)
    if pieces == 1:
        arrived, share = lax.optimization_barrier((arrived, share))
    shares = [share] + [swap(share, "col", 2 * k) for k in range(1, nz)]
    mine = call(sum_kernel, shape((2 * shard, width), real), arrived, 8)
    theirs = swap(mine, "col", 1)
    dagg, dends = call(
        latent_kernel, (shape((2 * shard, width), bf16), message),
        (mine, theirs, weight, body), 8,
    )
    dfar = swap_next(dends)
    scale = (shard * ncol * nrow) ** (-0.5)
    return call(
        functools.partial(final_kernel, scale),
        (shape(features.shape, bf16), shape(weight.shape, real)),
        (dagg, body, sib, dfar, *shares), 8,
    )


def solution(mesh):
    placed = (
        P(AXES, None),
        P(),
        P(AXES, None),
        P("row", "col", None),
        P("row", "col", None),
        P("row", "col", None),
        P("row", "col"),
        P("row", "col", None),
        P("row", "col", None),
    )
    return jax.shard_map(
        local, mesh=mesh, in_specs=placed, out_specs=(P(AXES, None), P()), check_vma=False
    )
```

```python
import functools

import jax
import jax.numpy as jnp
from jax import lax
from jax.experimental import pallas as pl
from jax.experimental.pallas import tpu as pltpu
from jax.sharding import PartitionSpec as P

BLOCK = 128
AXES = ("row", "col")
INV5 = -858993459
VMEM = pl.BlockSpec(memory_space=pltpu.VMEM)
SMEM = pl.BlockSpec(memory_space=pltpu.SMEM)
CHUNK_CELLS = 128
BOUNDS = (0, 18, 62, 64)


def params(mib):
    return pltpu.CompilerParams(vmem_limit_bytes=mib * 2**20)


def swap(x, axis, step):
    count = lax.axis_size(axis)
    return lax.ppermute(x, axis, [(i, i ^ step) for i in range(count)])


def swap_next(x):
    count = lax.axis_size("row") * lax.axis_size("col")
    pairs = []
    for s in range(1, count, 2):
        pairs += [(s, (s + 1) % count), ((s + 1) % count, s)]
    return lax.ppermute(x, AXES, pairs)


def inner(axis_end):
    chips = lax.axis_size("row") * lax.axis_size("col") // 2
    chip = (lax.axis_index("row") * lax.axis_size("col") + lax.axis_index("col")) // 2
    return jnp.where(chip == (chips - 1 if axis_end else 0), 0.0, 1.0).astype(jnp.float32)


def swap_mixed(x, step, along_z=0):
    nrow, ncol = lax.axis_size("row"), lax.axis_size("col")
    pairs = []
    for r in range(nrow):
        for c in range(ncol):
            if c % 2 == along_z and step < ncol // 2:
                pairs.append((r * ncol + c, r * ncol + (c ^ (2 * step))))
            if c % 2 != along_z and step < nrow:
                pairs.append((r * ncol + c, (r ^ step) * ncol + c))
    return lax.ppermute(x, AXES, pairs)


def stencil(values, link, prev, nxt):
    rows, width = values.shape
    node = lax.broadcasted_iota(jnp.int32, (rows, width), 0)
    before = jnp.where(node == 0, prev, pltpu.roll(values, 1, 0))
    after = jnp.where(node == rows - 1, nxt, pltpu.roll(link * values, rows - 1, 0))
    return 0.5 * values + 0.25 * (link * before + after)


def parity(even, odd):
    side = lax.rem(lax.axis_index("col"), 2)
    pl.when(side == 0)(even)
    pl.when(side == 1)(odd)


def cut_links(cuts_s, node):
    cut = node == cuts_s[0, 0]
    for t in range(1, cuts_s.shape[1]):
        cut = jnp.logical_or(cut, node == cuts_s[0, t])
    return jnp.where(cut, 0.0, 1.0).astype(jnp.float32)


def pinned(arrays):
    return [pltpu.with_memory_space_constraint(x, pltpu.HBM) for x in arrays]


def body_kernel(at, features_hbm, rows, cols, keys, nrows, ncols, cuts_hbm, *refs):
    body_ref, meta_ref, ends_ref, cuts_s, sems = refs
    shard, width = features_hbm.shape
    pairs = [(cuts_hbm, cuts_s), (features_hbm, body_ref.at[pl.ds(0, shard), :])]
    for source, spot in (
        (rows, at.rows), (cols, at.cols), (keys, at.keys), (nrows, at.nrows), (ncols, at.ncols),
    ):
        pairs.append((source.at[0], meta_ref.at[:, pl.ds(spot, source.shape[2])]))
    copies = [pltpu.make_async_copy(a, b, sems.at[t]) for t, (a, b) in enumerate(pairs)]
    for copy in copies:
        copy.start()
    copies[0].wait()
    link = cut_links(cuts_s, lax.broadcasted_iota(jnp.int32, (shard, width), 0))
    body_ref[shard:, :] = link.astype(body_ref.dtype)
    copies[1].wait()
    spot = lax.broadcasted_iota(jnp.int32, (16, width), 0)
    first = link[0:1] * body_ref[0:16, :].astype(jnp.float32)[0:1]
    tail = body_ref[shard - 16 : shard, :].astype(jnp.float32)
    rows = jnp.where(spot == 0, first, jnp.where(spot == 1, link[0:1], tail))
    ends_ref[...] = rows.astype(ends_ref.dtype)
    for copy in copies[2:]:
        copy.wait()


def bodies(at, features, slots, cuts):
    shard, width = features.shape
    arrays = pinned([features, *slots, cuts])
    return pl.pallas_call(
        functools.partial(body_kernel, at),
        out_shape=(
            jax.ShapeDtypeStruct((2 * shard, width), features.dtype),
            jax.ShapeDtypeStruct((1, at.end), jnp.int32),
            jax.ShapeDtypeStruct((16, width), features.dtype),
        ),
        in_specs=[pl.BlockSpec(memory_space=pltpu.HBM)] * len(arrays),
        out_specs=(VMEM, VMEM, VMEM),
        scratch_shapes=[
            pltpu.SMEM(cuts.shape, jnp.int32),
            pltpu.SemaphoreType.DMA((len(arrays),)),
        ],
        compiler_params=params(4),
    )(*arrays)


def pair_kernel(body_ref, sib_ref, far_ref, sib_far_ref, out_ref):
    shard = body_ref.shape[0] // 2

    def both(first_ref, second_ref, before_ref, after_ref):
        first = first_ref[0:shard, :].astype(jnp.float32)
        second = second_ref[0:shard, :].astype(jnp.float32)
        first_link = first_ref[shard:, :].astype(jnp.float32)
        second_link = second_ref[shard:, :].astype(jnp.float32)
        prev = before_ref[...].astype(jnp.float32)[15:16] * inner(False)
        nxt = after_ref[...].astype(jnp.float32)[0:1] * inner(True)
        head = second_link[0:1] * second[0:1]
        tail = first[shard - 1 : shard]
        out_ref[0:shard, :] = stencil(first, first_link, prev, head).astype(out_ref.dtype)
        out_ref[shard:, :] = stencil(second, second_link, tail, nxt).astype(out_ref.dtype)

    parity(
        lambda: both(body_ref, sib_ref, far_ref, sib_far_ref),
        lambda: both(sib_ref, body_ref, sib_far_ref, far_ref),
    )


class Slots:
    def __init__(self, slots, negatives):
        self.slots, self.negatives = slots, negatives
        self.rows, self.cols, self.keys = 0, slots, 2 * slots
        self.nrows = 3 * slots
        self.ncols = self.nrows + negatives
        self.end = self.ncols + negatives


def count_kernel(at, base, blocks, cols, per, meta_ref, count_s, n_ref):
    here_rows = per * 2 * (lax.axis_index("col") // 2)
    here_cols = per * lax.axis_index("row")
    width = cols * BLOCK
    total = jnp.zeros((blocks, width), jnp.float32)
    count = count_s[0, 0]
    for rows_at, cols_at, slots, positive in (
        (at.rows, at.cols, at.slots, True),
        (at.nrows, at.ncols, at.negatives, False),
    ):
        rows = jnp.bitwise_xor(meta_ref[0:1, rows_at : rows_at + slots], here_rows) - base
        cols_of = jnp.bitwise_xor(meta_ref[0:1, cols_at : cols_at + slots], here_cols)
        hit = lax.broadcasted_iota(jnp.int32, (blocks, slots), 0) == rows
        if positive:
            live = lax.broadcasted_iota(jnp.int32, (blocks, slots), 1) < count
            hit = jnp.logical_and(hit, live)
        lane = lax.shift_right_logical(lax.broadcasted_iota(jnp.int32, (width, slots), 0), 7)
        spread = jnp.where(lane == cols_of, 1.0, 0.0).astype(jnp.bfloat16)
        total += lax.dot_general(
            jnp.where(hit, 0.5, 0.0).astype(jnp.bfloat16), spread,
            (((1,), (1,)), ((), ())), preferred_element_type=jnp.float32,
        )
    n_ref[...] = total


def counts(at, base, blocks, cols, per, meta, count):
    return pl.pallas_call(
        functools.partial(count_kernel, at, base, blocks, cols, per),
        out_shape=jax.ShapeDtypeStruct((blocks, cols * BLOCK), jnp.float32),
        in_specs=[VMEM, SMEM],
        out_specs=VMEM,
        compiler_params=params(8),
    )(meta, count)


def target_kernel(at, base, blocks, cols, per, part, bounds, filtered, meta_s, count_s, *refs):
    t_ref, step_ref = refs[-2:]
    a = lax.broadcasted_iota(jnp.int32, (BLOCK, BLOCK), 0)
    b = lax.broadcasted_iota(jnp.int32, (BLOCK, BLOCK), 1)
    step_ref[...] = (a * BLOCK + b) * jnp.int32(4 * 40503)
    if part == 0:

        def clear(i, _):
            row = pl.multiple_of(i * BLOCK, BLOCK)
            t_ref[pl.ds(row, BLOCK), :] = jnp.zeros((BLOCK, cols * BLOCK), jnp.float32)
            return 0

        lax.fori_loop(0, blocks, clear, 0)
    here_rows = per * 2 * (lax.axis_index("col") // 2)
    here_cols = per * lax.axis_index("row")
    count = count_s[0, 0]
    unroll = 8 if at.slots % 8 == 0 else 1

    def positive(s):
        i = jnp.bitwise_xor(meta_s[0, at.rows + s], here_rows) - base
        j = jnp.bitwise_xor(meta_s[0, at.cols + s], here_cols)
        key = meta_s[0, at.keys + s] * 4
        one = jnp.where(s < count, 1.0, 0.0).astype(jnp.float32)

        def add():
            row = pl.multiple_of(i * BLOCK, BLOCK)
            col = pl.multiple_of(j * BLOCK, BLOCK)
            mixed = step_ref[...] + key
            mixed = jnp.bitwise_xor(mixed, lax.shift_right_logical(mixed, 11))
            fifth = lax.shift_right_logical(mixed, 9) * jnp.int32(INV5)
            hit = fifth.astype(jnp.uint32) < jnp.uint32(2**21)
            t_ref[pl.ds(row, BLOCK), pl.ds(col, BLOCK)] += jnp.where(hit, one, 0.0)

        if filtered:
            pl.when(jnp.logical_and(i >= 0, i < blocks))(add)
        else:
            add()

    def positives(g, _):
        for u in range(unroll):
            positive(g * unroll + u)
        return 0

    trips = (count + unroll - 1) // unroll
    first, last = bounds[part], bounds[part + 1]
    lax.fori_loop(trips * first // 64, trips * last // 64, positives, 0)


def targets(at, base, blocks, cols, per, part, bounds, filtered, meta, count, before):
    shape = (blocks * BLOCK, cols * BLOCK)
    old = [] if before is None else [before]
    return pl.pallas_call(
        functools.partial(target_kernel, at, base, blocks, cols, per, part, bounds, filtered),
        out_shape=jax.ShapeDtypeStruct(shape, jnp.float32),
        in_specs=[SMEM, SMEM] + [VMEM] * len(old),
        out_specs=VMEM,
        input_output_aliases={2: 0} if old else {},
        scratch_shapes=[pltpu.VMEM((BLOCK, BLOCK), jnp.int32)],
        compiler_params=params(10),
        cost_estimate=pl.CostEstimate(
            flops=at.slots * BLOCK * BLOCK * 4,
            bytes_accessed=at.slots * BLOCK * BLOCK * 4,
            transcendentals=0,
        ),
    )(meta, count, *old)


def decode_kernel(nz, nrow, first, count, refs):
    steps = max(nz, nrow) - 1
    t_ref, n_ref, weight_ref, pair_ref = refs[:4]
    recv = refs[4 : 4 + steps]
    other = refs[4 + steps : 4 + 2 * steps]
    refs = refs[4 + 2 * steps :]
    drow_ref, early_ref, late_ref, grad_ref, row_agg, col_agg, row_z = refs[:7]
    (col_z,) = refs[7:]
    split = early_ref.shape[0]
    pair = pair_ref.shape[0]
    shard = pair // 2
    columns = nrow * shard
    bf16 = jnp.bfloat16

    def gather(z_refs, row_refs, side):
        for k in range(count):
            ref = pair_ref if first + k == 0 else z_refs[first + k - 1]
            row_agg[k * pair : (k + 1) * pair, :] = ref[...]
        for q in range(nrow):
            ref = pair_ref if q == 0 else row_refs[q - 1]
            col_agg[q * shard : (q + 1) * shard, :] = ref[side * shard : (side + 1) * shard, :]

    parity(lambda: gather(recv, other, 0), lambda: gather(other, recv, 1))
    weight = weight_ref[...]
    dots = functools.partial(lax.dot_general, preferred_element_type=jnp.float32)
    nn = (((1,), (0,)), ((), ()))
    nt = (((1,), (1,)), ((), ()))
    tn = (((0,), (0,)), ((), ()))
    col_z[...] = dots(col_agg[...], weight, nn).astype(bf16)
    for k in range(count):
        at = slice(k * pair, (k + 1) * pair)
        row_z[at, :] = dots(row_agg[at, :], weight, nn).astype(bf16)
        half = row_z[at, :] * bf16(0.5)
        for c in range(0, columns, pair):
            cut = slice(c, min(c + pair, columns))
            curve = jnp.tanh(dots(half, col_z[cut, :], nt))
            for i in range(pair // BLOCK):
                row = k * pair + i * BLOCK
                n = n_ref[row // BLOCK : row // BLOCK + 1, cut]
                tile = t_ref[row : row + BLOCK, cut]
                part = n * curve[i * BLOCK : (i + 1) * BLOCK] + (n - tile)
                grad_ref[row : row + BLOCK, cut] = part.astype(bf16)
        drow = dots(grad_ref[at, :], col_z[...], nn) * (1.0 / 32.0)
        drow_ref[at, :] = drow
        low = k * pair
        if low < split:
            early_ref[at, :] = drow.astype(bf16)
        else:
            late_ref[low - split : low - split + pair, :] = drow.astype(bf16)


def column_kernel(
    nz, grad_ref, row_agg, col_agg, row_z, drow_ref, late_ref, dcol_ref, give_ref, share_ref
):
    dots = functools.partial(lax.dot_general, preferred_element_type=jnp.float32)
    nn = (((1,), (0,)), ((), ()))
    tn = (((0,), (0,)), ((), ()))
    bf16 = jnp.bfloat16
    columns = dcol_ref.shape[0]
    row_t = row_z[...].T
    step = min(columns, 4 * BLOCK)
    for c in range(0, columns, step):
        cut = slice(c, c + step)
        dcol = dots(row_t, grad_ref[:, cut], nn).T * (1.0 / 32.0)
        dcol_ref[cut, :] = dcol
    share = dots(row_agg[...], drow_ref[...].astype(bf16), tn)
    share += dots(col_agg[...], dcol_ref[...].astype(bf16), tn)
    share_ref[...] = share
    width = share.shape[0]
    body = give_ref.shape[0] - width - 16
    give_ref[body : body + width, :] = share.astype(bf16)
    rows = drow_ref.shape[0]
    pair = rows // nz
    z = lax.axis_index("col") // 2

    def first():
        give_ref[0:columns, :] = dcol_ref[...].astype(bf16)
        top = pl.multiple_of(z * pair, 8)
        bottom = pl.multiple_of(jnp.bitwise_xor(z, nz - 1) * pair + pair - 8, 8)
        edge = [drow_ref[pl.ds(top, 8), :], drow_ref[pl.ds(bottom, 8), :]]
        give_ref[body + width :, :] = jnp.concatenate(edge, axis=0).astype(bf16)

    def second():
        give_ref[0 : late_ref.shape[0], :] = late_ref[...]
        give_ref[body + width :, :] = jnp.zeros((16, share.shape[1]), bf16)

    parity(first, second)


def decode(t, n, weight, pair, recv, other, nz, nrow, first, count):
    rows, columns = t.shape
    width = weight.shape[1]
    bf16, real = jnp.bfloat16, jnp.float32
    shape = jax.ShapeDtypeStruct
    early = max(count // 2, 1)
    outs = [
        shape((rows, width), real),
        shape((early * rows // count, width), bf16),
        shape((max(count - early, 1) * rows // count, width), bf16),
        shape((rows, columns), bf16),
        shape((rows, width), bf16),
        shape((columns, width), bf16),
        shape((rows, width), bf16),
    ]
    return pl.pallas_call(
        lambda *refs: decode_kernel(nz, nrow, first, count, refs),
        out_shape=outs,
        in_specs=[VMEM] * (4 + len(recv) + len(other)),
        out_specs=[VMEM] * len(outs),
        scratch_shapes=[pltpu.VMEM((columns, width), bf16)],
        compiler_params=params(12),
        cost_estimate=pl.CostEstimate(
            flops=4 * rows * columns * width,
            bytes_accessed=rows * columns * 4,
            transcendentals=rows * columns,
        ),
    )(t, n, weight, pair, *recv, *other)


def column_parts(nz, parts, width):
    drow, early, late, grad, row_agg, col_agg, row_z = parts
    rows, columns = grad.shape
    bf16, real = jnp.bfloat16, jnp.float32
    shape = jax.ShapeDtypeStruct
    return call(
        functools.partial(column_kernel, nz),
        (
            shape((columns, width), real),
            shape((max(columns, rows // 2) + width + 16, width), bf16),
            shape((width, width), real),
        ),
        (grad, row_agg, col_agg, row_z, drow, late), 10,
    )


def merge_kernel(nz, nrow, drow_ref, dcol_ref, share_ref, early_ref, late_ref, *messages):
    width = share_ref.shape[0]
    half = width // 2
    pair = messages[0].shape[0] - half - 16
    shard = pair // 2
    bf16, real = jnp.bfloat16, jnp.float32
    r = lax.axis_index("row")
    z = lax.axis_index("col") // 2
    spot = lax.broadcasted_iota(jnp.int32, (16, width), 0)

    split = early_ref.shape[0]
    tail = late_ref.shape[0] - width - 16

    def rows_of_other(start, size):
        ref, start = (early_ref, start) if start < split else (late_ref, start - split)
        return ref[start : start + size, :].astype(real)

    def chip_row(k, low):
        row = 0 if low else pair - 1
        found = jnp.zeros((1, width), real)
        for t in range(nz):
            near = t * pair + (0 if low else pair - 16)
            at = row % 16 if not low else 0
            value = drow_ref[near : near + 16, :] + rows_of_other(near, 16)
            found = jnp.where(k == t, value[at : at + 1], found)
        return found

    def block(prev, nxt):
        return jnp.where(spot == 0, prev, jnp.where(spot == 8, nxt, 0.0)).astype(bf16)

    def on(flag):
        return jnp.where(flag, 1.0, 0.0).astype(real)

    def rows():
        share = share_ref[0:half, :] + late_ref[tail : tail + half, :].astype(real)
        for k in range(len(messages)):
            if k < nz:
                at = slice(k * pair, (k + 1) * pair)
                total = drow_ref[at, :] + rows_of_other(k * pair, pair)
                messages[k][0:pair, :] = total.astype(bf16)
            to = jnp.bitwise_xor(z, k)
            prev = jnp.bitwise_xor(jnp.maximum(to - 1, 0), z)
            nxt = jnp.bitwise_xor(jnp.minimum(to + 1, nz - 1), z)
            messages[k][pair : pair + half, :] = share.astype(bf16)
            messages[k][pair + half :, :] = block(
                chip_row(prev, False) * on(to > 0),
                chip_row(nxt, True) * on(to < nz - 1),
            )

    def columns():
        share = share_ref[half:, :] + late_ref[tail + half : tail + width, :].astype(real)
        edge = late_ref[tail + width :, :].astype(real)
        top = pl.multiple_of(z * pair, 8)
        bottom = pl.multiple_of(jnp.bitwise_xor(z, nz - 1) * pair + pair - 8, 8)
        first = drow_ref[pl.ds(top, 8), :][0:1] + edge[0:1]
        last = drow_ref[pl.ds(bottom, 8), :][7:8] + edge[15:16]
        for q in range(len(messages)):
            if q < nrow:
                at = slice(q * shard, (q + 1) * shard)
                messages[q][0:shard, :] = late_ref[at, :]
                messages[q][shard:pair, :] = dcol_ref[at, :].astype(bf16)
            to = jnp.bitwise_xor(r, q)
            before = jnp.bitwise_xor(jnp.maximum(to - 1, 0), r)
            after = jnp.bitwise_xor(jnp.minimum(to + 1, nrow - 1), r)
            mine = dcol_ref[pl.ds(pl.multiple_of(before * shard + shard - 8, 8), 8), :][7:8]
            theirs = late_ref[pl.ds(pl.multiple_of(after * shard, 16), 16), :][0:1]
            prev = last * on(r == to - 1) + mine * on(z == nz - 1)
            nxt = first * on(r == to + 1) + theirs.astype(real) * on(z == 0)
            messages[q][pair : pair + half, :] = share.astype(bf16)
            messages[q][pair + half :, :] = block(prev * on(to > 0), nxt * on(to < nrow - 1))

    parity(rows, columns)


def tree_sum(parts):
    parts = [x.astype(jnp.float32) for x in parts]
    while len(parts) > 1:
        parts = [a + b for a, b in zip(parts[::2], parts[1::2])]
    return parts[0]


def sum_kernel(*refs):
    mine_ref, on_ref = refs[-2:]
    half = on_ref.shape[0] - 32
    pair = mine_ref.shape[0] - half - 16
    total = tree_sum([x[...] for x in refs[:-2]])
    mine_ref[...] = total
    edge = jnp.concatenate([total[0:8], total[pair - 8 : pair]], axis=0)
    on_ref[...] = jnp.concatenate([total[pair:], edge], axis=0).astype(on_ref.dtype)


def last_kernel(nz, *refs):
    parts, out_ref = refs[:-1], refs[-1]
    half = parts[0].shape[0] - 32
    z = lax.axis_index("col") // 2
    total = tree_sum([x[0 : half + 16, :] for x in parts])
    out_ref[0:half, :] = total[0:half]
    spot = lax.broadcasted_iota(jnp.int32, (16, total.shape[1]), 0)
    prev = jnp.where(z == 0, total[half : half + 1], 0.0)
    nxt = jnp.where(z == nz - 1, total[half + 8 : half + 9], 0.0)
    for k in range(1, nz):
        edge = parts[k][half + 16 :, :].astype(jnp.float32)
        to = jnp.bitwise_xor(z, k)
        prev = jnp.where(to == z - 1, edge[15:16], prev)
        nxt = jnp.where(to == z + 1, edge[0:1], nxt)
    out_ref[half:, :] = jnp.where(spot == 0, prev, jnp.where(spot == 8, nxt, 0.0))


def back(dlatent, weight_ref):
    dagg = lax.dot_general(
        dlatent.astype(jnp.bfloat16), weight_ref[...], (((1,), (1,)), ((), ())),
        preferred_element_type=jnp.float32,
    )
    return dagg.astype(jnp.bfloat16).astype(jnp.float32)


def inner_kernel(mine_ref, theirs_ref, weight_ref, body_ref, sib_ref, out_ref):
    shard = out_ref.shape[0]
    pair = 2 * shard
    real = jnp.float32
    link = body_ref[shard:, :].astype(real)
    dagg = back(mine_ref[0:pair, :] + theirs_ref[0:pair, :], weight_ref)
    none = jnp.zeros((1, dagg.shape[1]), real)

    def even():
        nxt = sib_ref[shard : shard + 16, :].astype(real)[0:1] * dagg[shard : shard + 1]
        out_ref[...] = stencil(dagg[0:shard], link, none, nxt)

    def odd():
        out_ref[...] = stencil(dagg[shard:], link, dagg[shard - 1 : shard], none)

    parity(even, odd)


def final_kernel(
    scale, inner_ref, mine_ref, theirs_ref, last_ref, got_ref, weight_ref, body_ref, far_ref,
    features_ref, grad_ref,
):
    half = last_ref.shape[0] - 16
    shard = inner_ref.shape[0]
    at = mine_ref.shape[0] - 16
    real = jnp.float32
    kind = features_ref.dtype
    spot = lax.broadcasted_iota(jnp.int32, (16, inner_ref.shape[1]), 0)

    def even():
        near = back(mine_ref[at:, :] + got_ref[half:, :], weight_ref)[0:1]
        near = near * body_ref[shard : shard + 16, :].astype(real)[0:1]
        head = inner_ref[0:16, :] + jnp.where(spot == 0, 0.25 * near, 0.0)
        features_ref[0:16, :] = head.astype(kind)
        features_ref[16:, :] = inner_ref[16:, :].astype(kind)
        grad_ref[0:half, :] = last_ref[0:half, :] * scale
        grad_ref[half:, :] = got_ref[0:half, :] * scale

    def odd():
        near = back(theirs_ref[at:, :] + last_ref[half:, :], weight_ref)[8:9]
        near = near * far_ref[...].astype(real)[1:2]
        foot = inner_ref[shard - 16 :, :] + jnp.where(spot == 15, 0.25 * near, 0.0)
        features_ref[0 : shard - 16, :] = inner_ref[0 : shard - 16, :].astype(kind)
        features_ref[shard - 16 :, :] = foot.astype(kind)
        grad_ref[0:half, :] = got_ref[0:half, :] * scale
        grad_ref[half:, :] = last_ref[0:half, :] * scale

    parity(even, odd)


def call(kernel, outs, operands, mib, specs=None):
    return pl.pallas_call(
        kernel,
        out_shape=outs,
        in_specs=specs or [VMEM] * len(operands),
        out_specs=jax.tree.map(lambda _: VMEM, outs),
        compiler_params=params(mib),
    )(*operands)


def local(features, weight, cuts, pos_rows, pos_cols, pos_keys, pos_count, neg_rows, neg_cols):
    shard, width = features.shape
    ncol = lax.axis_size("col")
    nrow = lax.axis_size("row")
    nz = ncol // 2
    per = shard // BLOCK
    steps = max(nz, nrow)
    bf16, real = jnp.bfloat16, jnp.float32
    shape = jax.ShapeDtypeStruct

    at = Slots(pos_rows.shape[2], neg_rows.shape[2])
    slots = (pos_rows, pos_cols, pos_keys, neg_rows, neg_cols)
    body, meta, ends = bodies(at, features, slots, cuts)
    far = swap_next(ends)
    cols = nrow * per
    pieces = max(1, ncol * per * cols // CHUNK_CELLS)
    blocks = ncol * per // pieces
    bounds = BOUNDS if pieces == 1 else (0, 64)
    found = [
        targets(at, k * blocks, blocks, cols, per, 0, bounds, pieces > 1, meta, pos_count, None)
        for k in range(pieces)
    ]
    number = [counts(at, k * blocks, blocks, cols, per, meta, pos_count) for k in range(pieces)]
    if pieces == 1:
        far, found, number, body = lax.optimization_barrier((far, found, number, body))
    sib = swap(body, "col", 1)
    sib_far = swap(far, "col", 1)
    pair = call(pair_kernel, shape((2 * shard, width), bf16), (body, sib, far, sib_far), 4)
    recv = [swap_mixed(pair, k) for k in range(steps - 1, 0, -1)][::-1]
    if pieces == 1:
        t = targets(at, 0, blocks, cols, per, 1, bounds, False, meta, pos_count, found[0])
        recv, t = lax.optimization_barrier((recv, t))
        other = [swap(x, "col", 1) for x in recv]
        found = [targets(at, 0, blocks, cols, per, 2, bounds, False, meta, pos_count, t)]
    else:
        other = [swap(x, "col", 1) for x in recv]
    count = nz // pieces
    outs = [
        decode(t, n, weight, pair, recv, other, nz, nrow, k * count, count)
        for k, (t, n) in enumerate(zip(found, number))
    ]
    if pieces == 1:
        drow = outs[0][0]
        early = swap(outs[0][1], "col", 1)
        dcol, late, share = column_parts(nz, outs[0], width)
    else:
        found = [column_parts(count, x, width) for x in outs]
        drow = jnp.concatenate([x[0] for x in outs], axis=0)
        dcol, share = (tree_sum([x[k] for x in found]) for k in (0, 2))
        split = drow.shape[0] // 2
        early = swap(drow[0:split].astype(bf16), "col", 1)
        z = lax.axis_index("col") // 2
        pair_rows = drow.shape[0] // nz
        top = lax.dynamic_slice_in_dim(drow, z * pair_rows, 8)
        bottom = jnp.bitwise_xor(z, nz - 1) * pair_rows + pair_rows - 8
        edge = jnp.concatenate([top, lax.dynamic_slice_in_dim(drow, bottom, 8)], axis=0)
        long = max(dcol.shape[0], split)
        even = jnp.concatenate([dcol, jnp.zeros((long - dcol.shape[0], width), real)], axis=0)
        odd = jnp.concatenate([drow[split:], jnp.zeros((long - split, width), real)], axis=0)
        late = jnp.where(lax.rem(lax.axis_index("col"), 2) == 0, even, odd)
        late = jnp.concatenate([late, share, edge], axis=0).astype(bf16)
    late = swap(late, "col", 1)
    half = weight.shape[0] // 2
    messages = call(
        functools.partial(merge_kernel, nz, nrow),
        [shape((2 * shard + half + 16, width), bf16)] * steps,
        (drow, dcol, share, early, late), 8,
    )
    arrived = [swap_mixed(messages[k], k) for k in range(steps - 1, 0, -1)]
    mine, on = call(
        sum_kernel,
        (shape(messages[0].shape, real), shape((half + 32, width), bf16)),
        [messages[0]] + arrived[::-1], 8,
    )
    theirs = swap(mine, "col", 1)
    arrived = [swap_mixed(on, k, 1) for k in range(steps - 1, 0, -1)]
    last = call(
        functools.partial(last_kernel, nz), shape((half + 16, width), real),
        [on] + arrived[::-1], 4,
    )
    got = swap(last, "col", 1)
    inner_part = call(
        inner_kernel, shape(features.shape, real), (mine, theirs, weight, body, sib), 8
    )
    scale = (shard * ncol * nrow) ** (-0.5)
    return call(
        functools.partial(final_kernel, scale),
        (shape(features.shape, bf16), shape(weight.shape, real)),
        (inner_part, mine, theirs, last, got, weight, body, far), 8,
    )


def solution(mesh):
    placed = (
        P(AXES, None),
        P(),
        P(AXES, None),
        P("row", "col", None),
        P("row", "col", None),
        P("row", "col", None),
        P("row", "col"),
        P("row", "col", None),
        P("row", "col", None),
    )
    return jax.shard_map(
        local, mesh=mesh, in_specs=placed, out_specs=(P(AXES, None), P()), check_vma=False
    )
```

```python
import functools

import jax
import jax.numpy as jnp
from jax import lax
from jax.experimental import pallas as pl
from jax.experimental.pallas import tpu as pltpu
from jax.sharding import PartitionSpec as P

BLOCK = 128
AXES = ("row", "col")
INV5 = -858993459
VMEM = pl.BlockSpec(memory_space=pltpu.VMEM)
SMEM = pl.BlockSpec(memory_space=pltpu.SMEM)
CHUNK_CELLS = 128
BOUNDS = (0, 18, 62, 64)


def params(mib):
    return pltpu.CompilerParams(vmem_limit_bytes=mib * 2**20)


def swap(x, axis, step):
    count = lax.axis_size(axis)
    return lax.ppermute(x, axis, [(i, i ^ step) for i in range(count)])


def swap_next(x):
    count = lax.axis_size("row") * lax.axis_size("col")
    pairs = []
    for s in range(1, count, 2):
        pairs += [(s, (s + 1) % count), ((s + 1) % count, s)]
    return lax.ppermute(x, AXES, pairs)


def inner(axis_end):
    chips = lax.axis_size("row") * lax.axis_size("col") // 2
    chip = (lax.axis_index("row") * lax.axis_size("col") + lax.axis_index("col")) // 2
    return jnp.where(chip == (chips - 1 if axis_end else 0), 0.0, 1.0).astype(jnp.float32)


def swap_mixed(x, step, along_z=0):
    nrow, ncol = lax.axis_size("row"), lax.axis_size("col")
    pairs = []
    for r in range(nrow):
        for c in range(ncol):
            if c % 2 == along_z and step < ncol // 2:
                pairs.append((r * ncol + c, r * ncol + (c ^ (2 * step))))
            if c % 2 != along_z and step < nrow:
                pairs.append((r * ncol + c, (r ^ step) * ncol + c))
    return lax.ppermute(x, AXES, pairs)


def stencil(values, link, prev, nxt):
    rows, width = values.shape
    node = lax.broadcasted_iota(jnp.int32, (rows, width), 0)
    before = jnp.where(node == 0, prev, pltpu.roll(values, 1, 0))
    after = jnp.where(node == rows - 1, nxt, pltpu.roll(link * values, rows - 1, 0))
    return 0.5 * values + 0.25 * (link * before + after)


def parity(even, odd):
    side = lax.rem(lax.axis_index("col"), 2)
    pl.when(side == 0)(even)
    pl.when(side == 1)(odd)


def cut_links(cuts_s, node):
    cut = node == cuts_s[0, 0]
    for t in range(1, cuts_s.shape[1]):
        cut = jnp.logical_or(cut, node == cuts_s[0, t])
    return jnp.where(cut, 0.0, 1.0).astype(jnp.float32)


def pinned(arrays):
    return [pltpu.with_memory_space_constraint(x, pltpu.HBM) for x in arrays]


def body_kernel(at, features_hbm, rows, cols, keys, nrows, ncols, cuts_hbm, *refs):
    body_ref, meta_ref, ends_ref, cuts_s, sems = refs
    shard, width = features_hbm.shape
    pairs = [(cuts_hbm, cuts_s), (features_hbm, body_ref.at[pl.ds(0, shard), :])]
    for source, spot in (
        (rows, at.rows), (cols, at.cols), (keys, at.keys), (nrows, at.nrows), (ncols, at.ncols),
    ):
        pairs.append((source.at[0], meta_ref.at[:, pl.ds(spot, source.shape[2])]))
    copies = [pltpu.make_async_copy(a, b, sems.at[t]) for t, (a, b) in enumerate(pairs)]
    for copy in copies:
        copy.start()
    copies[0].wait()
    link = cut_links(cuts_s, lax.broadcasted_iota(jnp.int32, (shard, width), 0))
    body_ref[shard:, :] = link.astype(body_ref.dtype)
    copies[1].wait()
    spot = lax.broadcasted_iota(jnp.int32, (16, width), 0)
    first = link[0:1] * body_ref[0:16, :].astype(jnp.float32)[0:1]
    tail = body_ref[shard - 16 : shard, :].astype(jnp.float32)
    rows = jnp.where(spot == 0, first, jnp.where(spot == 1, link[0:1], tail))
    ends_ref[...] = rows.astype(ends_ref.dtype)
    for copy in copies[2:]:
        copy.wait()


def bodies(at, features, slots, cuts):
    shard, width = features.shape
    arrays = pinned([features, *slots, cuts])
    return pl.pallas_call(
        functools.partial(body_kernel, at),
        out_shape=(
            jax.ShapeDtypeStruct((2 * shard, width), features.dtype),
            jax.ShapeDtypeStruct((1, at.end), jnp.int32),
            jax.ShapeDtypeStruct((16, width), features.dtype),
        ),
        in_specs=[pl.BlockSpec(memory_space=pltpu.HBM)] * len(arrays),
        out_specs=(VMEM, VMEM, VMEM),
        scratch_shapes=[
            pltpu.SMEM(cuts.shape, jnp.int32),
            pltpu.SemaphoreType.DMA((len(arrays),)),
        ],
        compiler_params=params(4),
    )(*arrays)


def pair_kernel(body_ref, sib_ref, far_ref, sib_far_ref, out_ref):
    shard = body_ref.shape[0] // 2

    def both(first_ref, second_ref, before_ref, after_ref):
        first = first_ref[0:shard, :].astype(jnp.float32)
        second = second_ref[0:shard, :].astype(jnp.float32)
        first_link = first_ref[shard:, :].astype(jnp.float32)
        second_link = second_ref[shard:, :].astype(jnp.float32)
        prev = before_ref[...].astype(jnp.float32)[15:16] * inner(False)
        nxt = after_ref[...].astype(jnp.float32)[0:1] * inner(True)
        head = second_link[0:1] * second[0:1]
        tail = first[shard - 1 : shard]
        out_ref[0:shard, :] = stencil(first, first_link, prev, head).astype(out_ref.dtype)
        out_ref[shard:, :] = stencil(second, second_link, tail, nxt).astype(out_ref.dtype)

    parity(
        lambda: both(body_ref, sib_ref, far_ref, sib_far_ref),
        lambda: both(sib_ref, body_ref, sib_far_ref, far_ref),
    )


class Slots:
    def __init__(self, slots, negatives):
        self.slots, self.negatives = slots, negatives
        self.rows, self.cols, self.keys = 0, slots, 2 * slots
        self.nrows = 3 * slots
        self.ncols = self.nrows + negatives
        self.end = self.ncols + negatives


def count_kernel(at, base, blocks, cols, per, meta_ref, count_s, n_ref):
    here_rows = per * 2 * (lax.axis_index("col") // 2)
    here_cols = per * lax.axis_index("row")
    width = cols * BLOCK
    total = jnp.zeros((blocks, width), jnp.float32)
    count = count_s[0, 0]
    for rows_at, cols_at, slots, positive in (
        (at.rows, at.cols, at.slots, True),
        (at.nrows, at.ncols, at.negatives, False),
    ):
        rows = jnp.bitwise_xor(meta_ref[0:1, rows_at : rows_at + slots], here_rows) - base
        cols_of = jnp.bitwise_xor(meta_ref[0:1, cols_at : cols_at + slots], here_cols)
        hit = lax.broadcasted_iota(jnp.int32, (blocks, slots), 0) == rows
        if positive:
            live = lax.broadcasted_iota(jnp.int32, (blocks, slots), 1) < count
            hit = jnp.logical_and(hit, live)
        lane = lax.shift_right_logical(lax.broadcasted_iota(jnp.int32, (width, slots), 0), 7)
        spread = jnp.where(lane == cols_of, 1.0, 0.0).astype(jnp.bfloat16)
        total += lax.dot_general(
            jnp.where(hit, 0.5, 0.0).astype(jnp.bfloat16), spread,
            (((1,), (1,)), ((), ())), preferred_element_type=jnp.float32,
        )
    n_ref[...] = total


def counts(at, base, blocks, cols, per, meta, count):
    return pl.pallas_call(
        functools.partial(count_kernel, at, base, blocks, cols, per),
        out_shape=jax.ShapeDtypeStruct((blocks, cols * BLOCK), jnp.float32),
        in_specs=[VMEM, SMEM],
        out_specs=VMEM,
        compiler_params=params(8),
    )(meta, count)


def target_kernel(at, base, blocks, cols, per, part, bounds, filtered, meta_s, count_s, *refs):
    t_ref, step_ref = refs[-2:]
    a = lax.broadcasted_iota(jnp.int32, (BLOCK, BLOCK), 0)
    b = lax.broadcasted_iota(jnp.int32, (BLOCK, BLOCK), 1)
    step_ref[...] = (a * BLOCK + b) * jnp.int32(4 * 40503)
    if part == 0:

        def clear(i, _):
            row = pl.multiple_of(i * BLOCK, BLOCK)
            t_ref[pl.ds(row, BLOCK), :] = jnp.zeros((BLOCK, cols * BLOCK), jnp.float32)
            return 0

        lax.fori_loop(0, blocks, clear, 0)
    here_rows = per * 2 * (lax.axis_index("col") // 2)
    here_cols = per * lax.axis_index("row")
    count = count_s[0, 0]
    unroll = 8 if at.slots % 8 == 0 else 1

    def positive(s):
        i = jnp.bitwise_xor(meta_s[0, at.rows + s], here_rows) - base
        j = jnp.bitwise_xor(meta_s[0, at.cols + s], here_cols)
        key = meta_s[0, at.keys + s] * 4
        one = jnp.where(s < count, 1.0, 0.0).astype(jnp.float32)

        def add():
            row = pl.multiple_of(i * BLOCK, BLOCK)
            col = pl.multiple_of(j * BLOCK, BLOCK)
            mixed = step_ref[...] + key
            mixed = jnp.bitwise_xor(mixed, lax.shift_right_logical(mixed, 11))
            fifth = lax.shift_right_logical(mixed, 9) * jnp.int32(INV5)
            hit = fifth.astype(jnp.uint32) < jnp.uint32(2**21)
            t_ref[pl.ds(row, BLOCK), pl.ds(col, BLOCK)] += jnp.where(hit, one, 0.0)

        if filtered:
            pl.when(jnp.logical_and(i >= 0, i < blocks))(add)
        else:
            add()

    def positives(g, _):
        for u in range(unroll):
            positive(g * unroll + u)
        return 0

    trips = (count + unroll - 1) // unroll
    first, last = bounds[part], bounds[part + 1]
    lax.fori_loop(trips * first // 64, trips * last // 64, positives, 0)


def targets(at, base, blocks, cols, per, part, bounds, filtered, meta, count, before):
    shape = (blocks * BLOCK, cols * BLOCK)
    old = [] if before is None else [before]
    return pl.pallas_call(
        functools.partial(target_kernel, at, base, blocks, cols, per, part, bounds, filtered),
        out_shape=pltpu.VMEM(shape, jnp.float32),
        in_specs=[SMEM, SMEM] + [VMEM] * len(old),
        out_specs=VMEM,
        input_output_aliases={2: 0} if old else {},
        scratch_shapes=[pltpu.VMEM((BLOCK, BLOCK), jnp.int32)],
        compiler_params=params(10),
        cost_estimate=pl.CostEstimate(
            flops=at.slots * BLOCK * BLOCK * 4,
            bytes_accessed=at.slots * BLOCK * BLOCK * 4,
            transcendentals=0,
        ),
    )(meta, count, *old)


def decode_kernel(nz, nrow, first, count, refs):
    steps = max(nz, nrow) - 1
    t_ref, n_ref, weight_ref, pair_ref = refs[:4]
    recv = refs[4 : 4 + steps]
    other = refs[4 + steps : 4 + 2 * steps]
    refs = refs[4 + 2 * steps :]
    drow_ref, early_ref, late_ref, grad_ref, row_agg, col_agg, row_z = refs[:7]
    (col_z,) = refs[7:]
    split = early_ref.shape[0]
    pair = pair_ref.shape[0]
    shard = pair // 2
    columns = nrow * shard
    bf16 = jnp.bfloat16

    def gather(z_refs, row_refs, side):
        for k in range(count):
            ref = pair_ref if first + k == 0 else z_refs[first + k - 1]
            row_agg[k * pair : (k + 1) * pair, :] = ref[...]
        for q in range(nrow):
            ref = pair_ref if q == 0 else row_refs[q - 1]
            col_agg[q * shard : (q + 1) * shard, :] = ref[side * shard : (side + 1) * shard, :]

    parity(lambda: gather(recv, other, 0), lambda: gather(other, recv, 1))
    weight = weight_ref[...]
    dots = functools.partial(lax.dot_general, preferred_element_type=jnp.float32)
    nn = (((1,), (0,)), ((), ()))
    nt = (((1,), (1,)), ((), ()))
    tn = (((0,), (0,)), ((), ()))
    col_z[...] = dots(col_agg[...], weight, nn).astype(bf16)
    for k in range(count):
        at = slice(k * pair, (k + 1) * pair)
        row_z[at, :] = dots(row_agg[at, :], weight, nn).astype(bf16)
        half = row_z[at, :] * bf16(0.5)
        for c in range(0, columns, pair):
            cut = slice(c, min(c + pair, columns))
            curve = jnp.tanh(dots(half, col_z[cut, :], nt))
            for i in range(pair // BLOCK):
                row = k * pair + i * BLOCK
                n = n_ref[row // BLOCK : row // BLOCK + 1, cut]
                tile = t_ref[row : row + BLOCK, cut]
                part = n * curve[i * BLOCK : (i + 1) * BLOCK] + (n - tile)
                grad_ref[row : row + BLOCK, cut] = part.astype(bf16)
        drow = dots(grad_ref[at, :], col_z[...], nn) * (1.0 / 32.0)
        drow_ref[at, :] = drow
        low = k * pair
        if low < split:
            early_ref[at, :] = drow.astype(bf16)
        else:
            late_ref[low - split : low - split + pair, :] = drow.astype(bf16)


def column_kernel(
    nz, grad_ref, row_agg, col_agg, row_z, drow_ref, late_ref, dcol_ref, give_ref, share_ref
):
    dots = functools.partial(lax.dot_general, preferred_element_type=jnp.float32)
    nn = (((1,), (0,)), ((), ()))
    tn = (((0,), (0,)), ((), ()))
    bf16 = jnp.bfloat16
    columns = dcol_ref.shape[0]
    row_t = row_z[...].T
    step = min(columns, 4 * BLOCK)
    for c in range(0, columns, step):
        cut = slice(c, c + step)
        dcol = dots(row_t, grad_ref[:, cut], nn).T * (1.0 / 32.0)
        dcol_ref[cut, :] = dcol
    share = dots(row_agg[...], drow_ref[...].astype(bf16), tn)
    share += dots(col_agg[...], dcol_ref[...].astype(bf16), tn)
    share_ref[...] = share
    width = share.shape[0]
    body = give_ref.shape[0] - width - 16
    give_ref[body : body + width, :] = share.astype(bf16)
    rows = drow_ref.shape[0]
    pair = rows // nz
    z = lax.axis_index("col") // 2

    def first():
        give_ref[0:columns, :] = dcol_ref[...].astype(bf16)
        top = pl.multiple_of(z * pair, 8)
        bottom = pl.multiple_of(jnp.bitwise_xor(z, nz - 1) * pair + pair - 8, 8)
        edge = [drow_ref[pl.ds(top, 8), :], drow_ref[pl.ds(bottom, 8), :]]
        give_ref[body + width :, :] = jnp.concatenate(edge, axis=0).astype(bf16)

    def second():
        give_ref[0 : late_ref.shape[0], :] = late_ref[...]
        give_ref[body + width :, :] = jnp.zeros((16, share.shape[1]), bf16)

    parity(first, second)


def decode(t, n, weight, pair, recv, other, nz, nrow, first, count):
    rows, columns = t.shape
    width = weight.shape[1]
    bf16, real = jnp.bfloat16, jnp.float32
    shape = jax.ShapeDtypeStruct
    early = max(count // 2, 1)
    outs = [
        shape((rows, width), real),
        shape((early * rows // count, width), bf16),
        shape((max(count - early, 1) * rows // count, width), bf16),
        shape((rows, columns), bf16),
        shape((rows, width), bf16),
        shape((columns, width), bf16),
        shape((rows, width), bf16),
    ]
    return pl.pallas_call(
        lambda *refs: decode_kernel(nz, nrow, first, count, refs),
        out_shape=outs,
        in_specs=[VMEM] * (4 + len(recv) + len(other)),
        out_specs=[VMEM] * len(outs),
        scratch_shapes=[pltpu.VMEM((columns, width), bf16)],
        compiler_params=params(12),
        cost_estimate=pl.CostEstimate(
            flops=4 * rows * columns * width,
            bytes_accessed=rows * columns * 4,
            transcendentals=rows * columns,
        ),
    )(t, n, weight, pair, *recv, *other)


def column_parts(nz, parts, width):
    drow, early, late, grad, row_agg, col_agg, row_z = parts
    rows, columns = grad.shape
    bf16, real = jnp.bfloat16, jnp.float32
    shape = jax.ShapeDtypeStruct
    return call(
        functools.partial(column_kernel, nz),
        (
            shape((columns, width), real),
            shape((max(columns, rows // 2) + width + 16, width), bf16),
            shape((width, width), real),
        ),
        (grad, row_agg, col_agg, row_z, drow, late), 10,
    )


def merge_kernel(nz, nrow, drow_ref, dcol_ref, share_ref, early_ref, late_ref, *messages):
    width = share_ref.shape[0]
    half = width // 2
    pair = messages[0].shape[0] - half - 16
    shard = pair // 2
    bf16, real = jnp.bfloat16, jnp.float32
    r = lax.axis_index("row")
    z = lax.axis_index("col") // 2
    spot = lax.broadcasted_iota(jnp.int32, (16, width), 0)

    split = early_ref.shape[0]
    tail = late_ref.shape[0] - width - 16

    def rows_of_other(start, size):
        ref, start = (early_ref, start) if start < split else (late_ref, start - split)
        return ref[start : start + size, :].astype(real)

    def chip_row(k, low):
        row = 0 if low else pair - 1
        found = jnp.zeros((1, width), real)
        for t in range(nz):
            near = t * pair + (0 if low else pair - 16)
            at = row % 16 if not low else 0
            value = drow_ref[near : near + 16, :] + rows_of_other(near, 16)
            found = jnp.where(k == t, value[at : at + 1], found)
        return found

    def block(prev, nxt):
        return jnp.where(spot == 0, prev, jnp.where(spot == 8, nxt, 0.0)).astype(bf16)

    def on(flag):
        return jnp.where(flag, 1.0, 0.0).astype(real)

    def rows():
        share = share_ref[0:half, :] + late_ref[tail : tail + half, :].astype(real)
        for k in range(len(messages)):
            if k < nz:
                at = slice(k * pair, (k + 1) * pair)
                total = drow_ref[at, :] + rows_of_other(k * pair, pair)
                messages[k][0:pair, :] = total.astype(bf16)
            to = jnp.bitwise_xor(z, k)
            prev = jnp.bitwise_xor(jnp.maximum(to - 1, 0), z)
            nxt = jnp.bitwise_xor(jnp.minimum(to + 1, nz - 1), z)
            messages[k][pair : pair + half, :] = share.astype(bf16)
            messages[k][pair + half :, :] = block(
                chip_row(prev, False) * on(to > 0),
                chip_row(nxt, True) * on(to < nz - 1),
            )

    def columns():
        share = share_ref[half:, :] + late_ref[tail + half : tail + width, :].astype(real)
        edge = late_ref[tail + width :, :].astype(real)
        top = pl.multiple_of(z * pair, 8)
        bottom = pl.multiple_of(jnp.bitwise_xor(z, nz - 1) * pair + pair - 8, 8)
        first = drow_ref[pl.ds(top, 8), :][0:1] + edge[0:1]
        last = drow_ref[pl.ds(bottom, 8), :][7:8] + edge[15:16]
        for q in range(len(messages)):
            if q < nrow:
                at = slice(q * shard, (q + 1) * shard)
                messages[q][0:shard, :] = late_ref[at, :]
                messages[q][shard:pair, :] = dcol_ref[at, :].astype(bf16)
            to = jnp.bitwise_xor(r, q)
            before = jnp.bitwise_xor(jnp.maximum(to - 1, 0), r)
            after = jnp.bitwise_xor(jnp.minimum(to + 1, nrow - 1), r)
            mine = dcol_ref[pl.ds(pl.multiple_of(before * shard + shard - 8, 8), 8), :][7:8]
            theirs = late_ref[pl.ds(pl.multiple_of(after * shard, 16), 16), :][0:1]
            prev = last * on(r == to - 1) + mine * on(z == nz - 1)
            nxt = first * on(r == to + 1) + theirs.astype(real) * on(z == 0)
            messages[q][pair : pair + half, :] = share.astype(bf16)
            messages[q][pair + half :, :] = block(prev * on(to > 0), nxt * on(to < nrow - 1))

    parity(rows, columns)


def tree_sum(parts):
    parts = [x.astype(jnp.float32) for x in parts]
    while len(parts) > 1:
        parts = [a + b for a, b in zip(parts[::2], parts[1::2])]
    return parts[0]


def sum_kernel(*refs):
    mine_ref, on_ref = refs[-2:]
    half = on_ref.shape[0] - 32
    pair = mine_ref.shape[0] - half - 16
    total = tree_sum([x[...] for x in refs[:-2]])
    mine_ref[...] = total
    edge = jnp.concatenate([total[0:8], total[pair - 8 : pair]], axis=0)
    on_ref[...] = jnp.concatenate([total[pair:], edge], axis=0).astype(on_ref.dtype)


def last_kernel(nz, *refs):
    parts, out_ref = refs[:-1], refs[-1]
    half = parts[0].shape[0] - 32
    z = lax.axis_index("col") // 2
    total = tree_sum([x[0 : half + 16, :] for x in parts])
    out_ref[0:half, :] = total[0:half]
    spot = lax.broadcasted_iota(jnp.int32, (16, total.shape[1]), 0)
    prev = jnp.where(z == 0, total[half : half + 1], 0.0)
    nxt = jnp.where(z == nz - 1, total[half + 8 : half + 9], 0.0)
    for k in range(1, nz):
        edge = parts[k][half + 16 :, :].astype(jnp.float32)
        to = jnp.bitwise_xor(z, k)
        prev = jnp.where(to == z - 1, edge[15:16], prev)
        nxt = jnp.where(to == z + 1, edge[0:1], nxt)
    out_ref[half:, :] = jnp.where(spot == 0, prev, jnp.where(spot == 8, nxt, 0.0))


def back(dlatent, weight_ref):
    dagg = lax.dot_general(
        dlatent.astype(jnp.bfloat16), weight_ref[...], (((1,), (1,)), ((), ())),
        preferred_element_type=jnp.float32,
    )
    return dagg.astype(jnp.bfloat16).astype(jnp.float32)


def inner_kernel(mine_ref, theirs_ref, weight_ref, body_ref, sib_ref, out_ref):
    shard = out_ref.shape[0]
    pair = 2 * shard
    real = jnp.float32
    link = body_ref[shard:, :].astype(real)
    dagg = back(mine_ref[0:pair, :] + theirs_ref[0:pair, :], weight_ref)
    none = jnp.zeros((1, dagg.shape[1]), real)

    def even():
        nxt = sib_ref[shard : shard + 16, :].astype(real)[0:1] * dagg[shard : shard + 1]
        out_ref[...] = stencil(dagg[0:shard], link, none, nxt)

    def odd():
        out_ref[...] = stencil(dagg[shard:], link, dagg[shard - 1 : shard], none)

    parity(even, odd)


def final_kernel(
    scale, inner_ref, mine_ref, theirs_ref, last_ref, got_ref, weight_ref, body_ref, far_ref,
    features_ref, grad_ref,
):
    half = last_ref.shape[0] - 16
    shard = inner_ref.shape[0]
    at = mine_ref.shape[0] - 16
    real = jnp.float32
    kind = features_ref.dtype
    spot = lax.broadcasted_iota(jnp.int32, (16, inner_ref.shape[1]), 0)

    def even():
        near = back(mine_ref[at:, :] + got_ref[half:, :], weight_ref)[0:1]
        near = near * body_ref[shard : shard + 16, :].astype(real)[0:1]
        head = inner_ref[0:16, :] + jnp.where(spot == 0, 0.25 * near, 0.0)
        features_ref[0:16, :] = head.astype(kind)
        features_ref[16:, :] = inner_ref[16:, :].astype(kind)
        grad_ref[0:half, :] = last_ref[0:half, :] * scale
        grad_ref[half:, :] = got_ref[0:half, :] * scale

    def odd():
        near = back(theirs_ref[at:, :] + last_ref[half:, :], weight_ref)[8:9]
        near = near * far_ref[...].astype(real)[1:2]
        foot = inner_ref[shard - 16 :, :] + jnp.where(spot == 15, 0.25 * near, 0.0)
        features_ref[0 : shard - 16, :] = inner_ref[0 : shard - 16, :].astype(kind)
        features_ref[shard - 16 :, :] = foot.astype(kind)
        grad_ref[0:half, :] = got_ref[0:half, :] * scale
        grad_ref[half:, :] = last_ref[0:half, :] * scale

    parity(even, odd)


def call(kernel, outs, operands, mib, specs=None):
    return pl.pallas_call(
        kernel,
        out_shape=outs,
        in_specs=specs or [VMEM] * len(operands),
        out_specs=jax.tree.map(lambda _: VMEM, outs),
        compiler_params=params(mib),
    )(*operands)


def local(features, weight, cuts, pos_rows, pos_cols, pos_keys, pos_count, neg_rows, neg_cols):
    shard, width = features.shape
    ncol = lax.axis_size("col")
    nrow = lax.axis_size("row")
    nz = ncol // 2
    per = shard // BLOCK
    steps = max(nz, nrow)
    bf16, real = jnp.bfloat16, jnp.float32
    shape = jax.ShapeDtypeStruct

    at = Slots(pos_rows.shape[2], neg_rows.shape[2])
    slots = (pos_rows, pos_cols, pos_keys, neg_rows, neg_cols)
    body, meta, ends = bodies(at, features, slots, cuts)
    far = swap_next(ends)
    cols = nrow * per
    pieces = max(1, ncol * per * cols // CHUNK_CELLS)
    blocks = ncol * per // pieces
    bounds = BOUNDS if pieces == 1 else (0, 64)
    found = [
        targets(at, k * blocks, blocks, cols, per, 0, bounds, pieces > 1, meta, pos_count, None)
        for k in range(pieces)
    ]
    number = [counts(at, k * blocks, blocks, cols, per, meta, pos_count) for k in range(pieces)]
    if pieces == 1:
        far, found, number, body = lax.optimization_barrier((far, found, number, body))
    sib = swap(body, "col", 1)
    sib_far = swap(far, "col", 1)
    pair = call(pair_kernel, shape((2 * shard, width), bf16), (body, sib, far, sib_far), 4)
    recv = [swap_mixed(pair, k) for k in range(steps - 1, 0, -1)][::-1]
    if pieces == 1:
        t = targets(at, 0, blocks, cols, per, 1, bounds, False, meta, pos_count, found[0])
        recv, t = lax.optimization_barrier((recv, t))
        other = [swap(x, "col", 1) for x in recv]
        found = [targets(at, 0, blocks, cols, per, 2, bounds, False, meta, pos_count, t)]
    else:
        other = [swap(x, "col", 1) for x in recv]
    count = nz // pieces
    outs = [
        decode(t, n, weight, pair, recv, other, nz, nrow, k * count, count)
        for k, (t, n) in enumerate(zip(found, number))
    ]
    if pieces == 1:
        drow = outs[0][0]
        early = swap(outs[0][1], "col", 1)
        dcol, late, share = column_parts(nz, outs[0], width)
    else:
        found = [column_parts(count, x, width) for x in outs]
        drow = jnp.concatenate([x[0] for x in outs], axis=0)
        dcol, share = (tree_sum([x[k] for x in found]) for k in (0, 2))
        split = drow.shape[0] // 2
        early = swap(drow[0:split].astype(bf16), "col", 1)
        z = lax.axis_index("col") // 2
        pair_rows = drow.shape[0] // nz
        top = lax.dynamic_slice_in_dim(drow, z * pair_rows, 8)
        bottom = jnp.bitwise_xor(z, nz - 1) * pair_rows + pair_rows - 8
        edge = jnp.concatenate([top, lax.dynamic_slice_in_dim(drow, bottom, 8)], axis=0)
        long = max(dcol.shape[0], split)
        even = jnp.concatenate([dcol, jnp.zeros((long - dcol.shape[0], width), real)], axis=0)
        odd = jnp.concatenate([drow[split:], jnp.zeros((long - split, width), real)], axis=0)
        late = jnp.where(lax.rem(lax.axis_index("col"), 2) == 0, even, odd)
        late = jnp.concatenate([late, share, edge], axis=0).astype(bf16)
    late = swap(late, "col", 1)
    half = weight.shape[0] // 2
    messages = call(
        functools.partial(merge_kernel, nz, nrow),
        [shape((2 * shard + half + 16, width), bf16)] * steps,
        (drow, dcol, share, early, late), 8,
    )
    arrived = [swap_mixed(messages[k], k) for k in range(steps - 1, 0, -1)]
    mine, on = call(
        sum_kernel,
        (shape(messages[0].shape, real), shape((half + 32, width), bf16)),
        [messages[0]] + arrived[::-1], 8,
    )
    theirs = swap(mine, "col", 1)
    arrived = [swap_mixed(on, k, 1) for k in range(steps - 1, 0, -1)]
    last = call(
        functools.partial(last_kernel, nz), shape((half + 16, width), real),
        [on] + arrived[::-1], 4,
    )
    got = swap(last, "col", 1)
    inner_part = call(
        inner_kernel, shape(features.shape, real), (mine, theirs, weight, body, sib), 8
    )
    scale = (shard * ncol * nrow) ** (-0.5)
    return call(
        functools.partial(final_kernel, scale),
        (shape(features.shape, bf16), shape(weight.shape, real)),
        (inner_part, mine, theirs, last, got, weight, body, far), 8,
    )


def solution(mesh):
    placed = (
        P(AXES, None),
        P(),
        P(AXES, None),
        P("row", "col", None),
        P("row", "col", None),
        P("row", "col", None),
        P("row", "col"),
        P("row", "col", None),
        P("row", "col", None),
    )
    return jax.shard_map(
        local, mesh=mesh, in_specs=placed, out_specs=(P(AXES, None), P()), check_vma=False
    )
```

```python
import functools

import jax
import jax.numpy as jnp
from jax import lax
from jax.experimental import pallas as pl
from jax.experimental.pallas import tpu as pltpu
from jax.sharding import PartitionSpec as P

BLOCK = 128
AXES = ("row", "col")
INV5 = -858993459
VMEM = pl.BlockSpec(memory_space=pltpu.VMEM)
SMEM = pl.BlockSpec(memory_space=pltpu.SMEM)
CHUNK_CELLS = 128
BOUNDS = (0, 18, 62, 64)


def params(mib):
    return pltpu.CompilerParams(vmem_limit_bytes=mib * 2**20)


def swap(x, axis, step):
    count = lax.axis_size(axis)
    return lax.ppermute(x, axis, [(i, i ^ step) for i in range(count)])


def swap_next(x):
    count = lax.axis_size("row") * lax.axis_size("col")
    pairs = []
    for s in range(1, count, 2):
        pairs += [(s, (s + 1) % count), ((s + 1) % count, s)]
    return lax.ppermute(x, AXES, pairs)


def inner(axis_end):
    chips = lax.axis_size("row") * lax.axis_size("col") // 2
    chip = (lax.axis_index("row") * lax.axis_size("col") + lax.axis_index("col")) // 2
    return jnp.where(chip == (chips - 1 if axis_end else 0), 0.0, 1.0).astype(jnp.float32)


def swap_mixed(x, step, along_z=0):
    nrow, ncol = lax.axis_size("row"), lax.axis_size("col")
    pairs = []
    for r in range(nrow):
        for c in range(ncol):
            if c % 2 == along_z and step < ncol // 2:
                pairs.append((r * ncol + c, r * ncol + (c ^ (2 * step))))
            if c % 2 != along_z and step < nrow:
                pairs.append((r * ncol + c, (r ^ step) * ncol + c))
    return lax.ppermute(x, AXES, pairs)


def stencil(values, link, prev, nxt):
    rows, width = values.shape
    node = lax.broadcasted_iota(jnp.int32, (rows, width), 0)
    before = jnp.where(node == 0, prev, pltpu.roll(values, 1, 0))
    after = jnp.where(node == rows - 1, nxt, pltpu.roll(link * values, rows - 1, 0))
    return 0.5 * values + 0.25 * (link * before + after)


def parity(even, odd):
    side = lax.rem(lax.axis_index("col"), 2)
    pl.when(side == 0)(even)
    pl.when(side == 1)(odd)


def cut_links(cuts_s, node):
    cut = node == cuts_s[0, 0]
    for t in range(1, cuts_s.shape[1]):
        cut = jnp.logical_or(cut, node == cuts_s[0, t])
    return jnp.where(cut, 0.0, 1.0).astype(jnp.float32)


def pinned(arrays):
    return [pltpu.with_memory_space_constraint(x, pltpu.HBM) for x in arrays]


def body_kernel(at, features_hbm, rows, cols, keys, nrows, ncols, cuts_hbm, *refs):
    body_ref, meta_ref, ends_ref, cuts_s, sems = refs
    shard, width = features_hbm.shape
    pairs = [(cuts_hbm, cuts_s), (features_hbm, body_ref.at[pl.ds(0, shard), :])]
    for source, spot in (
        (rows, at.rows), (cols, at.cols), (keys, at.keys), (nrows, at.nrows), (ncols, at.ncols),
    ):
        pairs.append((source.at[0], meta_ref.at[:, pl.ds(spot, source.shape[2])]))
    copies = [pltpu.make_async_copy(a, b, sems.at[t]) for t, (a, b) in enumerate(pairs)]
    for copy in copies:
        copy.start()
    copies[0].wait()
    link = cut_links(cuts_s, lax.broadcasted_iota(jnp.int32, (shard, width), 0))
    body_ref[shard:, :] = link.astype(body_ref.dtype)
    copies[1].wait()
    spot = lax.broadcasted_iota(jnp.int32, (16, width), 0)
    first = link[0:1] * body_ref[0:16, :].astype(jnp.float32)[0:1]
    tail = body_ref[shard - 16 : shard, :].astype(jnp.float32)
    rows = jnp.where(spot == 0, first, jnp.where(spot == 1, link[0:1], tail))
    ends_ref[...] = rows.astype(ends_ref.dtype)
    for copy in copies[2:]:
        copy.wait()


def bodies(at, features, slots, cuts):
    shard, width = features.shape
    arrays = pinned([features, *slots, cuts])
    return pl.pallas_call(
        functools.partial(body_kernel, at),
        out_shape=(
            jax.ShapeDtypeStruct((2 * shard, width), features.dtype),
            jax.ShapeDtypeStruct((1, at.end), jnp.int32),
            jax.ShapeDtypeStruct((16, width), features.dtype),
        ),
        in_specs=[pl.BlockSpec(memory_space=pltpu.HBM)] * len(arrays),
        out_specs=(VMEM, VMEM, VMEM),
        scratch_shapes=[
            pltpu.SMEM(cuts.shape, jnp.int32),
            pltpu.SemaphoreType.DMA((len(arrays),)),
        ],
        compiler_params=params(4),
    )(*arrays)


def pair_kernel(body_ref, sib_ref, far_ref, sib_far_ref, out_ref):
    shard = body_ref.shape[0] // 2

    def both(first_ref, second_ref, before_ref, after_ref):
        first = first_ref[0:shard, :].astype(jnp.float32)
        second = second_ref[0:shard, :].astype(jnp.float32)
        first_link = first_ref[shard:, :].astype(jnp.float32)
        second_link = second_ref[shard:, :].astype(jnp.float32)
        prev = before_ref[...].astype(jnp.float32)[15:16] * inner(False)
        nxt = after_ref[...].astype(jnp.float32)[0:1] * inner(True)
        head = second_link[0:1] * second[0:1]
        tail = first[shard - 1 : shard]
        out_ref[0:shard, :] = stencil(first, first_link, prev, head).astype(out_ref.dtype)
        out_ref[shard:, :] = stencil(second, second_link, tail, nxt).astype(out_ref.dtype)

    parity(
        lambda: both(body_ref, sib_ref, far_ref, sib_far_ref),
        lambda: both(sib_ref, body_ref, sib_far_ref, far_ref),
    )


class Slots:
    def __init__(self, slots, negatives):
        self.slots, self.negatives = slots, negatives
        self.rows, self.cols, self.keys = 0, slots, 2 * slots
        self.nrows = 3 * slots
        self.ncols = self.nrows + negatives
        self.end = self.ncols + negatives


def count_kernel(at, base, blocks, cols, per, meta_ref, count_s, n_ref):
    here_rows = per * 2 * (lax.axis_index("col") // 2)
    here_cols = per * lax.axis_index("row")
    width = cols * BLOCK
    total = jnp.zeros((blocks, width), jnp.float32)
    count = count_s[0, 0]
    for rows_at, cols_at, slots, positive in (
        (at.rows, at.cols, at.slots, True),
        (at.nrows, at.ncols, at.negatives, False),
    ):
        rows = jnp.bitwise_xor(meta_ref[0:1, rows_at : rows_at + slots], here_rows) - base
        cols_of = jnp.bitwise_xor(meta_ref[0:1, cols_at : cols_at + slots], here_cols)
        hit = lax.broadcasted_iota(jnp.int32, (blocks, slots), 0) == rows
        if positive:
            live = lax.broadcasted_iota(jnp.int32, (blocks, slots), 1) < count
            hit = jnp.logical_and(hit, live)
        lane = lax.shift_right_logical(lax.broadcasted_iota(jnp.int32, (width, slots), 0), 7)
        spread = jnp.where(lane == cols_of, 1.0, 0.0).astype(jnp.bfloat16)
        total += lax.dot_general(
            jnp.where(hit, 0.5, 0.0).astype(jnp.bfloat16), spread,
            (((1,), (1,)), ((), ())), preferred_element_type=jnp.float32,
        )
    n_ref[...] = total


def counts(at, base, blocks, cols, per, meta, count):
    return pl.pallas_call(
        functools.partial(count_kernel, at, base, blocks, cols, per),
        out_shape=jax.ShapeDtypeStruct((blocks, cols * BLOCK), jnp.float32),
        in_specs=[VMEM, SMEM],
        out_specs=VMEM,
        compiler_params=params(8),
    )(meta, count)


def target_kernel(at, base, blocks, cols, per, part, bounds, filtered, meta_s, count_s, *refs):
    t_ref, step_ref = refs[-2:]
    a = lax.broadcasted_iota(jnp.int32, (BLOCK, BLOCK), 0)
    b = lax.broadcasted_iota(jnp.int32, (BLOCK, BLOCK), 1)
    step_ref[...] = (a * BLOCK + b) * jnp.int32(4 * 40503)
    if part == 0:

        def clear(i, _):
            row = pl.multiple_of(i * BLOCK, BLOCK)
            t_ref[pl.ds(row, BLOCK), :] = jnp.zeros((BLOCK, cols * BLOCK), jnp.float32)
            return 0

        lax.fori_loop(0, blocks, clear, 0)
    here_rows = per * 2 * (lax.axis_index("col") // 2)
    here_cols = per * lax.axis_index("row")
    count = count_s[0, 0]
    unroll = 8 if at.slots % 8 == 0 else 1

    def positive(s):
        i = jnp.bitwise_xor(meta_s[0, at.rows + s], here_rows) - base
        j = jnp.bitwise_xor(meta_s[0, at.cols + s], here_cols)
        key = meta_s[0, at.keys + s] * 4
        one = jnp.where(s < count, 1.0, 0.0).astype(jnp.float32)

        def add():
            row = pl.multiple_of(i * BLOCK, BLOCK)
            col = pl.multiple_of(j * BLOCK, BLOCK)
            mixed = step_ref[...] + key
            mixed = jnp.bitwise_xor(mixed, lax.shift_right_logical(mixed, 11))
            fifth = lax.shift_right_logical(mixed, 9) * jnp.int32(INV5)
            hit = fifth.astype(jnp.uint32) < jnp.uint32(2**21)
            t_ref[pl.ds(row, BLOCK), pl.ds(col, BLOCK)] += jnp.where(hit, one, 0.0)

        if filtered:
            pl.when(jnp.logical_and(i >= 0, i < blocks))(add)
        else:
            add()

    def positives(g, _):
        for u in range(unroll):
            positive(g * unroll + u)
        return 0

    trips = (count + unroll - 1) // unroll
    first, last = bounds[part], bounds[part + 1]
    lax.fori_loop(trips * first // 64, trips * last // 64, positives, 0)


def targets(at, base, blocks, cols, per, part, bounds, filtered, meta, count, before):
    shape = (blocks * BLOCK, cols * BLOCK)
    old = [] if before is None else [before]
    return pl.pallas_call(
        functools.partial(target_kernel, at, base, blocks, cols, per, part, bounds, filtered),
        out_shape=pltpu.VMEM(shape, jnp.float32),
        in_specs=[SMEM, SMEM] + [VMEM] * len(old),
        out_specs=VMEM,
        input_output_aliases={2: 0} if old else {},
        scratch_shapes=[pltpu.VMEM((BLOCK, BLOCK), jnp.int32)],
        compiler_params=params(10),
        cost_estimate=pl.CostEstimate(
            flops=at.slots * BLOCK * BLOCK * 4,
            bytes_accessed=at.slots * BLOCK * BLOCK * 4,
            transcendentals=0,
        ),
    )(meta, count, *old)


def decode_kernel(nz, nrow, first, count, refs):
    steps = max(nz, nrow) - 1
    t_ref, n_ref, weight_ref, pair_ref = refs[:4]
    recv = refs[4 : 4 + steps]
    other = refs[4 + steps : 4 + 2 * steps]
    refs = refs[4 + 2 * steps :]
    drow_ref, grad_ref, row_agg, col_agg, row_z = refs[:5]
    (col_z,) = refs[5:]
    pair = pair_ref.shape[0]
    shard = pair // 2
    columns = nrow * shard
    bf16 = jnp.bfloat16

    def gather(z_refs, row_refs, side):
        for k in range(count):
            ref = pair_ref if first + k == 0 else z_refs[first + k - 1]
            row_agg[k * pair : (k + 1) * pair, :] = ref[...]
        for q in range(nrow):
            ref = pair_ref if q == 0 else row_refs[q - 1]
            col_agg[q * shard : (q + 1) * shard, :] = ref[side * shard : (side + 1) * shard, :]

    parity(lambda: gather(recv, other, 0), lambda: gather(other, recv, 1))
    weight = weight_ref[...]
    dots = functools.partial(lax.dot_general, preferred_element_type=jnp.float32)
    nn = (((1,), (0,)), ((), ()))
    nt = (((1,), (1,)), ((), ()))
    tn = (((0,), (0,)), ((), ()))
    col_z[...] = dots(col_agg[...], weight, nn).astype(bf16)
    for k in range(count):
        at = slice(k * pair, (k + 1) * pair)
        row_z[at, :] = dots(row_agg[at, :], weight, nn).astype(bf16)
        half = row_z[at, :] * bf16(0.5)
        for c in range(0, columns, pair):
            cut = slice(c, min(c + pair, columns))
            curve = jnp.tanh(dots(half, col_z[cut, :], nt))
            for i in range(pair // BLOCK):
                row = k * pair + i * BLOCK
                n = n_ref[row // BLOCK : row // BLOCK + 1, cut]
                tile = t_ref[row : row + BLOCK, cut]
                part = n * curve[i * BLOCK : (i + 1) * BLOCK] + (n - tile)
                grad_ref[row : row + BLOCK, cut] = part.astype(bf16)
        drow = dots(grad_ref[at, :], col_z[...], nn) * (1.0 / 32.0)
        drow_ref[at, :] = drow


def column_kernel(
    nz, grad_ref, row_agg, col_agg, row_z, drow_ref, dcol_ref, give_ref, share_ref
):
    dots = functools.partial(lax.dot_general, preferred_element_type=jnp.float32)
    nn = (((1,), (0,)), ((), ()))
    tn = (((0,), (0,)), ((), ()))
    bf16 = jnp.bfloat16
    columns = dcol_ref.shape[0]
    row_t = row_z[...].T
    step = min(columns, 4 * BLOCK)
    for c in range(0, columns, step):
        cut = slice(c, c + step)
        dcol = dots(row_t, grad_ref[:, cut], nn).T * (1.0 / 32.0)
        dcol_ref[cut, :] = dcol
    share = dots(row_agg[...], drow_ref[...].astype(bf16), tn)
    share += dots(col_agg[...], dcol_ref[...].astype(bf16), tn)
    share_ref[...] = share
    width = share.shape[0]
    body = give_ref.shape[0] - width - 16
    give_ref[body : body + width, :] = share.astype(bf16)
    rows = drow_ref.shape[0]
    pair = rows // nz
    z = lax.axis_index("col") // 2

    def first():
        give_ref[0:columns, :] = dcol_ref[...].astype(bf16)
        top = pl.multiple_of(z * pair, 8)
        bottom = pl.multiple_of(jnp.bitwise_xor(z, nz - 1) * pair + pair - 8, 8)
        edge = [drow_ref[pl.ds(top, 8), :], drow_ref[pl.ds(bottom, 8), :]]
        give_ref[body + width :, :] = jnp.concatenate(edge, axis=0).astype(bf16)

    def second():
        give_ref[0:rows, :] = drow_ref[...].astype(bf16)
        give_ref[body + width :, :] = jnp.zeros((16, share.shape[1]), bf16)

    parity(first, second)


def decode(t, n, weight, pair, recv, other, nz, nrow, first, count):
    rows, columns = t.shape
    width = weight.shape[1]
    bf16, real = jnp.bfloat16, jnp.float32
    shape = jax.ShapeDtypeStruct
    outs = [
        shape((rows, width), real),
        shape((rows, columns), bf16),
        shape((rows, width), bf16),
        shape((columns, width), bf16),
        shape((rows, width), bf16),
    ]
    return pl.pallas_call(
        lambda *refs: decode_kernel(nz, nrow, first, count, refs),
        out_shape=outs,
        in_specs=[VMEM] * (4 + len(recv) + len(other)),
        out_specs=[VMEM] * len(outs),
        scratch_shapes=[pltpu.VMEM((columns, width), bf16)],
        compiler_params=params(12),
        cost_estimate=pl.CostEstimate(
            flops=4 * rows * columns * width,
            bytes_accessed=rows * columns * 4,
            transcendentals=rows * columns,
        ),
    )(t, n, weight, pair, *recv, *other)


def column_parts(nz, parts, width):
    drow, grad, row_agg, col_agg, row_z = parts
    rows, columns = grad.shape
    bf16, real = jnp.bfloat16, jnp.float32
    shape = jax.ShapeDtypeStruct
    return call(
        functools.partial(column_kernel, nz),
        (
            shape((columns, width), real),
            shape((max(columns, rows) + width + 16, width), bf16),
            shape((width, width), real),
        ),
        (grad, row_agg, col_agg, row_z, drow), 10,
    )


def merge_kernel(nz, nrow, drow_ref, dcol_ref, share_ref, late_ref, *messages):
    width = share_ref.shape[0]
    half = width // 2
    pair = messages[0].shape[0] - half - 16
    shard = pair // 2
    bf16, real = jnp.bfloat16, jnp.float32
    r = lax.axis_index("row")
    z = lax.axis_index("col") // 2
    spot = lax.broadcasted_iota(jnp.int32, (16, width), 0)

    tail = late_ref.shape[0] - width - 16

    def rows_of_other(start, size):
        return late_ref[start : start + size, :].astype(real)

    def chip_row(k, low):
        row = 0 if low else pair - 1
        found = jnp.zeros((1, width), real)
        for t in range(nz):
            near = t * pair + (0 if low else pair - 16)
            at = row % 16 if not low else 0
            value = drow_ref[near : near + 16, :] + rows_of_other(near, 16)
            found = jnp.where(k == t, value[at : at + 1], found)
        return found

    def block(prev, nxt):
        return jnp.where(spot == 0, prev, jnp.where(spot == 8, nxt, 0.0)).astype(bf16)

    def on(flag):
        return jnp.where(flag, 1.0, 0.0).astype(real)

    def rows():
        share = share_ref[0:half, :] + late_ref[tail : tail + half, :].astype(real)
        for k in range(len(messages)):
            if k < nz:
                at = slice(k * pair, (k + 1) * pair)
                total = drow_ref[at, :] + rows_of_other(k * pair, pair)
                messages[k][0:pair, :] = total.astype(bf16)
            to = jnp.bitwise_xor(z, k)
            prev = jnp.bitwise_xor(jnp.maximum(to - 1, 0), z)
            nxt = jnp.bitwise_xor(jnp.minimum(to + 1, nz - 1), z)
            messages[k][pair : pair + half, :] = share.astype(bf16)
            messages[k][pair + half :, :] = block(
                chip_row(prev, False) * on(to > 0),
                chip_row(nxt, True) * on(to < nz - 1),
            )

    def columns():
        share = share_ref[half:, :] + late_ref[tail + half : tail + width, :].astype(real)
        edge = late_ref[tail + width :, :].astype(real)
        top = pl.multiple_of(z * pair, 8)
        bottom = pl.multiple_of(jnp.bitwise_xor(z, nz - 1) * pair + pair - 8, 8)
        first = drow_ref[pl.ds(top, 8), :][0:1] + edge[0:1]
        last = drow_ref[pl.ds(bottom, 8), :][7:8] + edge[15:16]
        for q in range(len(messages)):
            if q < nrow:
                at = slice(q * shard, (q + 1) * shard)
                messages[q][0:shard, :] = late_ref[at, :]
                messages[q][shard:pair, :] = dcol_ref[at, :].astype(bf16)
            to = jnp.bitwise_xor(r, q)
            before = jnp.bitwise_xor(jnp.maximum(to - 1, 0), r)
            after = jnp.bitwise_xor(jnp.minimum(to + 1, nrow - 1), r)
            mine = dcol_ref[pl.ds(pl.multiple_of(before * shard + shard - 8, 8), 8), :][7:8]
            theirs = late_ref[pl.ds(pl.multiple_of(after * shard, 16), 16), :][0:1]
            prev = last * on(r == to - 1) + mine * on(z == nz - 1)
            nxt = first * on(r == to + 1) + theirs.astype(real) * on(z == 0)
            messages[q][pair : pair + half, :] = share.astype(bf16)
            messages[q][pair + half :, :] = block(prev * on(to > 0), nxt * on(to < nrow - 1))

    parity(rows, columns)


def tree_sum(parts):
    parts = [x.astype(jnp.float32) for x in parts]
    while len(parts) > 1:
        parts = [a + b for a, b in zip(parts[::2], parts[1::2])]
    return parts[0]


def sum_kernel(*refs):
    mine_ref, on_ref = refs[-2:]
    half = on_ref.shape[0] - 32
    pair = mine_ref.shape[0] - half - 16
    total = tree_sum([x[...] for x in refs[:-2]])
    mine_ref[...] = total
    edge = jnp.concatenate([total[0:8], total[pair - 8 : pair]], axis=0)
    on_ref[...] = jnp.concatenate([total[pair:], edge], axis=0).astype(on_ref.dtype)


def last_kernel(nz, *refs):
    parts, out_ref = refs[:-1], refs[-1]
    half = parts[0].shape[0] - 32
    z = lax.axis_index("col") // 2
    total = tree_sum([x[0 : half + 16, :] for x in parts])
    out_ref[0:half, :] = total[0:half]
    spot = lax.broadcasted_iota(jnp.int32, (16, total.shape[1]), 0)
    prev = jnp.where(z == 0, total[half : half + 1], 0.0)
    nxt = jnp.where(z == nz - 1, total[half + 8 : half + 9], 0.0)
    for k in range(1, nz):
        edge = parts[k][half + 16 :, :].astype(jnp.float32)
        to = jnp.bitwise_xor(z, k)
        prev = jnp.where(to == z - 1, edge[15:16], prev)
        nxt = jnp.where(to == z + 1, edge[0:1], nxt)
    out_ref[half:, :] = jnp.where(spot == 0, prev, jnp.where(spot == 8, nxt, 0.0))


def back(dlatent, weight_ref):
    dagg = lax.dot_general(
        dlatent.astype(jnp.bfloat16), weight_ref[...], (((1,), (1,)), ((), ())),
        preferred_element_type=jnp.float32,
    )
    return dagg.astype(jnp.bfloat16).astype(jnp.float32)


def inner_kernel(mine_ref, theirs_ref, weight_ref, body_ref, sib_ref, out_ref):
    shard = out_ref.shape[0]
    pair = 2 * shard
    real = jnp.float32
    link = body_ref[shard:, :].astype(real)
    dagg = back(mine_ref[0:pair, :] + theirs_ref[0:pair, :], weight_ref)
    none = jnp.zeros((1, dagg.shape[1]), real)

    def even():
        nxt = sib_ref[shard : shard + 16, :].astype(real)[0:1] * dagg[shard : shard + 1]
        out_ref[...] = stencil(dagg[0:shard], link, none, nxt)

    def odd():
        out_ref[...] = stencil(dagg[shard:], link, dagg[shard - 1 : shard], none)

    parity(even, odd)


def final_kernel(
    scale, inner_ref, mine_ref, theirs_ref, last_ref, got_ref, weight_ref, body_ref, far_ref,
    features_ref, grad_ref,
):
    half = last_ref.shape[0] - 16
    shard = inner_ref.shape[0]
    at = mine_ref.shape[0] - 16
    real = jnp.float32
    kind = features_ref.dtype
    spot = lax.broadcasted_iota(jnp.int32, (16, inner_ref.shape[1]), 0)

    def even():
        near = back(mine_ref[at:, :] + got_ref[half:, :], weight_ref)[0:1]
        near = near * body_ref[shard : shard + 16, :].astype(real)[0:1]
        head = inner_ref[0:16, :] + jnp.where(spot == 0, 0.25 * near, 0.0)
        features_ref[0:16, :] = head.astype(kind)
        features_ref[16:, :] = inner_ref[16:, :].astype(kind)
        grad_ref[0:half, :] = last_ref[0:half, :] * scale
        grad_ref[half:, :] = got_ref[0:half, :] * scale

    def odd():
        near = back(theirs_ref[at:, :] + last_ref[half:, :], weight_ref)[8:9]
        near = near * far_ref[...].astype(real)[1:2]
        foot = inner_ref[shard - 16 :, :] + jnp.where(spot == 15, 0.25 * near, 0.0)
        features_ref[0 : shard - 16, :] = inner_ref[0 : shard - 16, :].astype(kind)
        features_ref[shard - 16 :, :] = foot.astype(kind)
        grad_ref[0:half, :] = got_ref[0:half, :] * scale
        grad_ref[half:, :] = last_ref[0:half, :] * scale

    parity(even, odd)


def call(kernel, outs, operands, mib, specs=None):
    return pl.pallas_call(
        kernel,
        out_shape=outs,
        in_specs=specs or [VMEM] * len(operands),
        out_specs=jax.tree.map(lambda _: VMEM, outs),
        compiler_params=params(mib),
    )(*operands)


def local(features, weight, cuts, pos_rows, pos_cols, pos_keys, pos_count, neg_rows, neg_cols):
    shard, width = features.shape
    ncol = lax.axis_size("col")
    nrow = lax.axis_size("row")
    nz = ncol // 2
    per = shard // BLOCK
    steps = max(nz, nrow)
    bf16, real = jnp.bfloat16, jnp.float32
    shape = jax.ShapeDtypeStruct

    at = Slots(pos_rows.shape[2], neg_rows.shape[2])
    slots = (pos_rows, pos_cols, pos_keys, neg_rows, neg_cols)
    body, meta, ends = bodies(at, features, slots, cuts)
    far = swap_next(ends)
    cols = nrow * per
    pieces = max(1, ncol * per * cols // CHUNK_CELLS)
    blocks = ncol * per // pieces
    bounds = BOUNDS if pieces == 1 else (0, 64)
    found = [
        targets(at, k * blocks, blocks, cols, per, 0, bounds, pieces > 1, meta, pos_count, None)
        for k in range(pieces)
    ]
    number = [counts(at, k * blocks, blocks, cols, per, meta, pos_count) for k in range(pieces)]
    if pieces == 1:
        far, found, number, body = lax.optimization_barrier((far, found, number, body))
    sib = swap(body, "col", 1)
    sib_far = swap(far, "col", 1)
    pair = call(pair_kernel, shape((2 * shard, width), bf16), (body, sib, far, sib_far), 4)
    recv = [swap_mixed(pair, k) for k in range(steps - 1, 0, -1)][::-1]
    if pieces == 1:
        t = targets(at, 0, blocks, cols, per, 1, bounds, False, meta, pos_count, found[0])
        recv, t = lax.optimization_barrier((recv, t))
        other = [swap(x, "col", 1) for x in recv]
        found = [targets(at, 0, blocks, cols, per, 2, bounds, False, meta, pos_count, t)]
    else:
        other = [swap(x, "col", 1) for x in recv]
    count = nz // pieces
    outs = [
        decode(t, n, weight, pair, recv, other, nz, nrow, k * count, count)
        for k, (t, n) in enumerate(zip(found, number))
    ]
    if pieces == 1:
        drow = outs[0][0]
        dcol, late, share = column_parts(nz, outs[0], width)
    else:
        found = [column_parts(count, x, width) for x in outs]
        drow = jnp.concatenate([x[0] for x in outs], axis=0)
        dcol, share = (tree_sum([x[k] for x in found]) for k in (0, 2))
        z = lax.axis_index("col") // 2
        pair_rows = drow.shape[0] // nz
        top = lax.dynamic_slice_in_dim(drow, z * pair_rows, 8)
        bottom = jnp.bitwise_xor(z, nz - 1) * pair_rows + pair_rows - 8
        edge = jnp.concatenate([top, lax.dynamic_slice_in_dim(drow, bottom, 8)], axis=0)
        long = max(dcol.shape[0], drow.shape[0])
        even = jnp.concatenate([dcol, jnp.zeros((long - dcol.shape[0], width), real)], axis=0)
        odd = jnp.concatenate([drow, jnp.zeros((long - drow.shape[0], width), real)], axis=0)
        late = jnp.where(lax.rem(lax.axis_index("col"), 2) == 0, even, odd)
        late = jnp.concatenate([late, share, edge], axis=0).astype(bf16)
    late = swap(late, "col", 1)
    half = weight.shape[0] // 2
    messages = call(
        functools.partial(merge_kernel, nz, nrow),
        [shape((2 * shard + half + 16, width), bf16)] * steps,
        (drow, dcol, share, late), 8,
    )
    arrived = [swap_mixed(messages[k], k) for k in range(steps - 1, 0, -1)]
    mine, on = call(
        sum_kernel,
        (shape(messages[0].shape, real), shape((half + 32, width), bf16)),
        [messages[0]] + arrived[::-1], 8,
    )
    theirs = swap(mine, "col", 1)
    arrived = [swap_mixed(on, k, 1) for k in range(steps - 1, 0, -1)]
    last = call(
        functools.partial(last_kernel, nz), shape((half + 16, width), real),
        [on] + arrived[::-1], 4,
    )
    got = swap(last, "col", 1)
    inner_part = call(
        inner_kernel, shape(features.shape, real), (mine, theirs, weight, body, sib), 8
    )
    scale = (shard * ncol * nrow) ** (-0.5)
    return call(
        functools.partial(final_kernel, scale),
        (shape(features.shape, bf16), shape(weight.shape, real)),
        (inner_part, mine, theirs, last, got, weight, body, far), 8,
    )


def solution(mesh):
    placed = (
        P(AXES, None),
        P(),
        P(AXES, None),
        P("row", "col", None),
        P("row", "col", None),
        P("row", "col", None),
        P("row", "col"),
        P("row", "col", None),
        P("row", "col", None),
    )
    return jax.shard_map(
        local, mesh=mesh, in_specs=placed, out_specs=(P(AXES, None), P()), check_vma=False
    )
```

```python
import functools

import jax
import jax.numpy as jnp
from jax import lax
from jax.experimental import pallas as pl
from jax.experimental.pallas import tpu as pltpu
from jax.sharding import PartitionSpec as P

BLOCK = 128
AXES = ("row", "col")
INV5 = -858993459
VMEM = pl.BlockSpec(memory_space=pltpu.VMEM)
SMEM = pl.BlockSpec(memory_space=pltpu.SMEM)
CHUNK_CELLS = 128
BOUNDS = (0, 18, 62, 64)


def params(mib):
    return pltpu.CompilerParams(vmem_limit_bytes=mib * 2**20)


def swap(x, axis, step):
    count = lax.axis_size(axis)
    return lax.ppermute(x, axis, [(i, i ^ step) for i in range(count)])


def swap_next(x):
    count = lax.axis_size("row") * lax.axis_size("col")
    pairs = []
    for s in range(1, count, 2):
        pairs += [(s, (s + 1) % count), ((s + 1) % count, s)]
    return lax.ppermute(x, AXES, pairs)


def inner(axis_end):
    chips = lax.axis_size("row") * lax.axis_size("col") // 2
    chip = (lax.axis_index("row") * lax.axis_size("col") + lax.axis_index("col")) // 2
    return jnp.where(chip == (chips - 1 if axis_end else 0), 0.0, 1.0).astype(jnp.float32)


def swap_mixed(x, step, along_z=0):
    nrow, ncol = lax.axis_size("row"), lax.axis_size("col")
    pairs = []
    for r in range(nrow):
        for c in range(ncol):
            if c % 2 == along_z and step < ncol // 2:
                pairs.append((r * ncol + c, r * ncol + (c ^ (2 * step))))
            if c % 2 != along_z and step < nrow:
                pairs.append((r * ncol + c, (r ^ step) * ncol + c))
    return lax.ppermute(x, AXES, pairs)


def stencil(values, link, prev, nxt):
    rows, width = values.shape
    node = lax.broadcasted_iota(jnp.int32, (rows, width), 0)
    before = jnp.where(node == 0, prev, pltpu.roll(values, 1, 0))
    after = jnp.where(node == rows - 1, nxt, pltpu.roll(link * values, rows - 1, 0))
    return 0.5 * values + 0.25 * (link * before + after)


def parity(even, odd):
    side = lax.rem(lax.axis_index("col"), 2)
    pl.when(side == 0)(even)
    pl.when(side == 1)(odd)


def cut_links(cuts_s, node):
    cut = node == cuts_s[0, 0]
    for t in range(1, cuts_s.shape[1]):
        cut = jnp.logical_or(cut, node == cuts_s[0, t])
    return jnp.where(cut, 0.0, 1.0).astype(jnp.float32)


def pinned(arrays):
    return [pltpu.with_memory_space_constraint(x, pltpu.HBM) for x in arrays]


def body_kernel(at, features_hbm, rows, cols, keys, nrows, ncols, cuts_hbm, *refs):
    body_ref, meta_ref, ends_ref, cuts_s, sems = refs
    shard, width = features_hbm.shape
    pairs = [(cuts_hbm, cuts_s), (features_hbm, body_ref.at[pl.ds(0, shard), :])]
    for source, spot in (
        (rows, at.rows), (cols, at.cols), (keys, at.keys), (nrows, at.nrows), (ncols, at.ncols),
    ):
        pairs.append((source.at[0], meta_ref.at[:, pl.ds(spot, source.shape[2])]))
    copies = [pltpu.make_async_copy(a, b, sems.at[t]) for t, (a, b) in enumerate(pairs)]
    for copy in copies:
        copy.start()
    copies[0].wait()
    link = cut_links(cuts_s, lax.broadcasted_iota(jnp.int32, (shard, width), 0))
    body_ref[shard:, :] = link.astype(body_ref.dtype)
    copies[1].wait()
    spot = lax.broadcasted_iota(jnp.int32, (16, width), 0)
    first = link[0:1] * body_ref[0:16, :].astype(jnp.float32)[0:1]
    tail = body_ref[shard - 16 : shard, :].astype(jnp.float32)
    rows = jnp.where(spot == 0, first, jnp.where(spot == 1, link[0:1], tail))
    ends_ref[...] = rows.astype(ends_ref.dtype)
    for copy in copies[2:]:
        copy.wait()


def bodies(at, features, slots, cuts):
    shard, width = features.shape
    arrays = pinned([features, *slots, cuts])
    return pl.pallas_call(
        functools.partial(body_kernel, at),
        out_shape=(
            jax.ShapeDtypeStruct((2 * shard, width), features.dtype),
            jax.ShapeDtypeStruct((1, at.end), jnp.int32),
            jax.ShapeDtypeStruct((16, width), features.dtype),
        ),
        in_specs=[pl.BlockSpec(memory_space=pltpu.HBM)] * len(arrays),
        out_specs=(VMEM, VMEM, VMEM),
        scratch_shapes=[
            pltpu.SMEM(cuts.shape, jnp.int32),
            pltpu.SemaphoreType.DMA((len(arrays),)),
        ],
        compiler_params=params(4),
    )(*arrays)


def pair_kernel(body_ref, sib_ref, far_ref, sib_far_ref, out_ref):
    shard = body_ref.shape[0] // 2

    def both(first_ref, second_ref, before_ref, after_ref):
        first = first_ref[0:shard, :].astype(jnp.float32)
        second = second_ref[0:shard, :].astype(jnp.float32)
        first_link = first_ref[shard:, :].astype(jnp.float32)
        second_link = second_ref[shard:, :].astype(jnp.float32)
        prev = before_ref[...].astype(jnp.float32)[15:16] * inner(False)
        nxt = after_ref[...].astype(jnp.float32)[0:1] * inner(True)
        head = second_link[0:1] * second[0:1]
        tail = first[shard - 1 : shard]
        out_ref[0:shard, :] = stencil(first, first_link, prev, head).astype(out_ref.dtype)
        out_ref[shard:, :] = stencil(second, second_link, tail, nxt).astype(out_ref.dtype)

    parity(
        lambda: both(body_ref, sib_ref, far_ref, sib_far_ref),
        lambda: both(sib_ref, body_ref, sib_far_ref, far_ref),
    )


class Slots:
    def __init__(self, slots, negatives):
        self.slots, self.negatives = slots, negatives
        self.rows, self.cols, self.keys = 0, slots, 2 * slots
        self.nrows = 3 * slots
        self.ncols = self.nrows + negatives
        self.end = self.ncols + negatives


def count_kernel(at, base, blocks, cols, per, meta_ref, count_s, n_ref):
    here_rows = per * 2 * (lax.axis_index("col") // 2)
    here_cols = per * lax.axis_index("row")
    width = cols * BLOCK
    total = jnp.zeros((blocks, width), jnp.float32)
    count = count_s[0, 0]
    for rows_at, cols_at, slots, positive in (
        (at.rows, at.cols, at.slots, True),
        (at.nrows, at.ncols, at.negatives, False),
    ):
        rows = jnp.bitwise_xor(meta_ref[0:1, rows_at : rows_at + slots], here_rows) - base
        cols_of = jnp.bitwise_xor(meta_ref[0:1, cols_at : cols_at + slots], here_cols)
        hit = lax.broadcasted_iota(jnp.int32, (blocks, slots), 0) == rows
        if positive:
            live = lax.broadcasted_iota(jnp.int32, (blocks, slots), 1) < count
            hit = jnp.logical_and(hit, live)
        lane = lax.shift_right_logical(lax.broadcasted_iota(jnp.int32, (width, slots), 0), 7)
        spread = jnp.where(lane == cols_of, 1.0, 0.0).astype(jnp.bfloat16)
        total += lax.dot_general(
            jnp.where(hit, 0.5, 0.0).astype(jnp.bfloat16), spread,
            (((1,), (1,)), ((), ())), preferred_element_type=jnp.float32,
        )
    n_ref[...] = total


def counts(at, base, blocks, cols, per, meta, count):
    return pl.pallas_call(
        functools.partial(count_kernel, at, base, blocks, cols, per),
        out_shape=jax.ShapeDtypeStruct((blocks, cols * BLOCK), jnp.float32),
        in_specs=[VMEM, SMEM],
        out_specs=VMEM,
        compiler_params=params(8),
    )(meta, count)


def target_kernel(at, base, blocks, cols, per, part, bounds, filtered, meta_s, count_s, *refs):
    t_ref, step_ref = refs[-2:]
    a = lax.broadcasted_iota(jnp.int32, (BLOCK, BLOCK), 0)
    b = lax.broadcasted_iota(jnp.int32, (BLOCK, BLOCK), 1)
    step_ref[...] = (a * BLOCK + b) * jnp.int32(4 * 40503)
    if part == 0:

        def clear(i, _):
            row = pl.multiple_of(i * BLOCK, BLOCK)
            t_ref[pl.ds(row, BLOCK), :] = jnp.zeros((BLOCK, cols * BLOCK), jnp.float32)
            return 0

        lax.fori_loop(0, blocks, clear, 0)
    here_rows = per * 2 * (lax.axis_index("col") // 2)
    here_cols = per * lax.axis_index("row")
    count = count_s[0, 0]
    unroll = 8 if at.slots % 8 == 0 else 1

    def positive(s):
        i = jnp.bitwise_xor(meta_s[0, at.rows + s], here_rows) - base
        j = jnp.bitwise_xor(meta_s[0, at.cols + s], here_cols)
        key = meta_s[0, at.keys + s] * 4
        one = jnp.where(s < count, 1.0, 0.0).astype(jnp.float32)

        def add():
            row = pl.multiple_of(i * BLOCK, BLOCK)
            col = pl.multiple_of(j * BLOCK, BLOCK)
            mixed = step_ref[...] + key
            mixed = jnp.bitwise_xor(mixed, lax.shift_right_logical(mixed, 11))
            fifth = lax.shift_right_logical(mixed, 9) * jnp.int32(INV5)
            hit = fifth.astype(jnp.uint32) < jnp.uint32(2**21)
            t_ref[pl.ds(row, BLOCK), pl.ds(col, BLOCK)] += jnp.where(hit, one, 0.0)

        if filtered:
            pl.when(jnp.logical_and(i >= 0, i < blocks))(add)
        else:
            add()

    def positives(g, _):
        for u in range(unroll):
            positive(g * unroll + u)
        return 0

    trips = (count + unroll - 1) // unroll
    first, last = bounds[part], bounds[part + 1]
    lax.fori_loop(trips * first // 64, trips * last // 64, positives, 0)


def targets(at, base, blocks, cols, per, part, bounds, filtered, meta, count, before):
    shape = (blocks * BLOCK, cols * BLOCK)
    old = [] if before is None else [before]
    return pl.pallas_call(
        functools.partial(target_kernel, at, base, blocks, cols, per, part, bounds, filtered),
        out_shape=pltpu.VMEM(shape, jnp.float32),
        in_specs=[SMEM, SMEM] + [VMEM] * len(old),
        out_specs=VMEM,
        input_output_aliases={2: 0} if old else {},
        scratch_shapes=[pltpu.VMEM((BLOCK, BLOCK), jnp.int32)],
        compiler_params=params(10),
        cost_estimate=pl.CostEstimate(
            flops=at.slots * BLOCK * BLOCK * 4,
            bytes_accessed=at.slots * BLOCK * BLOCK * 4,
            transcendentals=0,
        ),
    )(meta, count, *old)


def decode_kernel(nz, nrow, first, count, refs):
    steps = max(nz, nrow) - 1
    t_ref, n_ref, weight_ref, pair_ref = refs[:4]
    recv = refs[4 : 4 + steps]
    other = refs[4 + steps : 4 + 2 * steps]
    refs = refs[4 + 2 * steps :]
    drow_ref, early_ref, late_ref, grad_ref, row_agg, col_agg, row_z = refs[:7]
    (col_z,) = refs[7:]
    split = early_ref.shape[0]
    pair = pair_ref.shape[0]
    shard = pair // 2
    columns = nrow * shard
    bf16 = jnp.bfloat16

    def gather(z_refs, row_refs, side):
        for k in range(count):
            ref = pair_ref if first + k == 0 else z_refs[first + k - 1]
            row_agg[k * pair : (k + 1) * pair, :] = ref[...]
        for q in range(nrow):
            ref = pair_ref if q == 0 else row_refs[q - 1]
            col_agg[q * shard : (q + 1) * shard, :] = ref[side * shard : (side + 1) * shard, :]

    parity(lambda: gather(recv, other, 0), lambda: gather(other, recv, 1))
    weight = weight_ref[...]
    dots = functools.partial(lax.dot_general, preferred_element_type=jnp.float32)
    nn = (((1,), (0,)), ((), ()))
    nt = (((1,), (1,)), ((), ()))
    tn = (((0,), (0,)), ((), ()))
    col_z[...] = dots(col_agg[...], weight, nn).astype(bf16)
    for k in range(count):
        at = slice(k * pair, (k + 1) * pair)
        row_z[at, :] = dots(row_agg[at, :], weight, nn).astype(bf16)
        half = row_z[at, :] * bf16(0.5)
        for c in range(0, columns, pair):
            cut = slice(c, min(c + pair, columns))
            curve = jnp.tanh(dots(half, col_z[cut, :], nt))
            for i in range(pair // BLOCK):
                row = k * pair + i * BLOCK
                n = n_ref[row // BLOCK : row // BLOCK + 1, cut]
                tile = t_ref[row : row + BLOCK, cut]
                part = n * curve[i * BLOCK : (i + 1) * BLOCK] + (n - tile)
                grad_ref[row : row + BLOCK, cut] = part.astype(bf16)
        drow = dots(grad_ref[at, :], col_z[...], nn) * (1.0 / 32.0)
        drow_ref[at, :] = drow.astype(bf16)
        low = k * pair
        if low < split:
            early_ref[at, :] = drow.astype(bf16)
        else:
            late_ref[low - split : low - split + pair, :] = drow.astype(bf16)


def column_kernel(
    nz, grad_ref, row_agg, col_agg, row_z, drow_ref, late_ref, dcol_ref, give_ref, share_ref
):
    dots = functools.partial(lax.dot_general, preferred_element_type=jnp.float32)
    nn = (((1,), (0,)), ((), ()))
    tn = (((0,), (0,)), ((), ()))
    bf16 = jnp.bfloat16
    columns = dcol_ref.shape[0]
    row_t = row_z[...].T
    step = min(columns, 4 * BLOCK)
    for c in range(0, columns, step):
        cut = slice(c, c + step)
        dcol = dots(row_t, grad_ref[:, cut], nn).T * (1.0 / 32.0)
        dcol_ref[cut, :] = dcol
    share = dots(row_agg[...], drow_ref[...], tn)
    share += dots(col_agg[...], dcol_ref[...].astype(bf16), tn)
    share_ref[...] = share
    width = share.shape[0]
    body = give_ref.shape[0] - width - 16
    give_ref[body : body + width, :] = share.astype(bf16)
    rows = drow_ref.shape[0]
    pair = rows // nz
    z = lax.axis_index("col") // 2

    def first():
        give_ref[0:columns, :] = dcol_ref[...].astype(bf16)
        top = pl.multiple_of(z * pair, 16)
        bottom = pl.multiple_of(jnp.bitwise_xor(z, nz - 1) * pair + pair - 16, 16)
        edge = [drow_ref[pl.ds(top, 16), :], drow_ref[pl.ds(bottom, 16), :]]
        edge = [edge[0].astype(jnp.float32)[0:8], edge[1].astype(jnp.float32)[8:16]]
        give_ref[body + width :, :] = jnp.concatenate(edge, axis=0).astype(bf16)

    def second():
        give_ref[0 : late_ref.shape[0], :] = late_ref[...]
        give_ref[body + width :, :] = jnp.zeros((16, share.shape[1]), bf16)

    parity(first, second)


def decode(t, n, weight, pair, recv, other, nz, nrow, first, count):
    rows, columns = t.shape
    width = weight.shape[1]
    bf16, real = jnp.bfloat16, jnp.float32
    shape = jax.ShapeDtypeStruct
    early = max(count // 2, 1)
    outs = [
        shape((rows, width), bf16),
        shape((early * rows // count, width), bf16),
        shape((max(count - early, 1) * rows // count, width), bf16),
        shape((rows, columns), bf16),
        shape((rows, width), bf16),
        shape((columns, width), bf16),
        shape((rows, width), bf16),
    ]
    return pl.pallas_call(
        lambda *refs: decode_kernel(nz, nrow, first, count, refs),
        out_shape=outs,
        in_specs=[VMEM] * (4 + len(recv) + len(other)),
        out_specs=[VMEM] * len(outs),
        scratch_shapes=[pltpu.VMEM((columns, width), bf16)],
        compiler_params=params(12),
        cost_estimate=pl.CostEstimate(
            flops=4 * rows * columns * width,
            bytes_accessed=rows * columns * 4,
            transcendentals=rows * columns,
        ),
    )(t, n, weight, pair, *recv, *other)


def column_parts(nz, parts, width):
    drow, early, late, grad, row_agg, col_agg, row_z = parts
    rows, columns = grad.shape
    bf16, real = jnp.bfloat16, jnp.float32
    shape = jax.ShapeDtypeStruct
    return call(
        functools.partial(column_kernel, nz),
        (
            shape((columns, width), real),
            shape((max(columns, rows // 2) + width + 16, width), bf16),
            shape((width, width), real),
        ),
        (grad, row_agg, col_agg, row_z, drow, late), 10,
    )


def merge_kernel(nz, nrow, drow_ref, dcol_ref, share_ref, early_ref, late_ref, *messages):
    width = share_ref.shape[0]
    half = width // 2
    pair = messages[0].shape[0] - half - 16
    shard = pair // 2
    bf16, real = jnp.bfloat16, jnp.float32
    r = lax.axis_index("row")
    z = lax.axis_index("col") // 2
    spot = lax.broadcasted_iota(jnp.int32, (16, width), 0)

    split = early_ref.shape[0]
    tail = late_ref.shape[0] - width - 16

    def rows_of_other(start, size):
        ref, start = (early_ref, start) if start < split else (late_ref, start - split)
        return ref[start : start + size, :].astype(real)

    def chip_row(k, low):
        row = 0 if low else pair - 1
        found = jnp.zeros((1, width), real)
        for t in range(nz):
            near = t * pair + (0 if low else pair - 16)
            at = row % 16 if not low else 0
            value = drow_ref[near : near + 16, :].astype(real) + rows_of_other(near, 16)
            found = jnp.where(k == t, value[at : at + 1], found)
        return found

    def block(prev, nxt):
        return jnp.where(spot == 0, prev, jnp.where(spot == 8, nxt, 0.0)).astype(bf16)

    def on(flag):
        return jnp.where(flag, 1.0, 0.0).astype(real)

    def rows():
        share = share_ref[0:half, :] + late_ref[tail : tail + half, :].astype(real)
        for k in range(len(messages)):
            if k < nz:
                at = slice(k * pair, (k + 1) * pair)
                total = drow_ref[at, :].astype(real) + rows_of_other(k * pair, pair)
                messages[k][0:pair, :] = total.astype(bf16)
            to = jnp.bitwise_xor(z, k)
            prev = jnp.bitwise_xor(jnp.maximum(to - 1, 0), z)
            nxt = jnp.bitwise_xor(jnp.minimum(to + 1, nz - 1), z)
            messages[k][pair : pair + half, :] = share.astype(bf16)
            messages[k][pair + half :, :] = block(
                chip_row(prev, False) * on(to > 0),
                chip_row(nxt, True) * on(to < nz - 1),
            )

    def columns():
        share = share_ref[half:, :] + late_ref[tail + half : tail + width, :].astype(real)
        edge = late_ref[tail + width :, :].astype(real)
        top = pl.multiple_of(z * pair, 16)
        bottom = pl.multiple_of(jnp.bitwise_xor(z, nz - 1) * pair + pair - 16, 16)
        first = drow_ref[pl.ds(top, 16), :].astype(real)[0:1] + edge[0:1]
        last = drow_ref[pl.ds(bottom, 16), :].astype(real)[15:16] + edge[15:16]
        for q in range(len(messages)):
            if q < nrow:
                at = slice(q * shard, (q + 1) * shard)
                messages[q][0:shard, :] = late_ref[at, :]
                messages[q][shard:pair, :] = dcol_ref[at, :].astype(bf16)
            to = jnp.bitwise_xor(r, q)
            before = jnp.bitwise_xor(jnp.maximum(to - 1, 0), r)
            after = jnp.bitwise_xor(jnp.minimum(to + 1, nrow - 1), r)
            mine = dcol_ref[pl.ds(pl.multiple_of(before * shard + shard - 8, 8), 8), :][7:8]
            theirs = late_ref[pl.ds(pl.multiple_of(after * shard, 16), 16), :][0:1]
            prev = last * on(r == to - 1) + mine * on(z == nz - 1)
            nxt = first * on(r == to + 1) + theirs.astype(real) * on(z == 0)
            messages[q][pair : pair + half, :] = share.astype(bf16)
            messages[q][pair + half :, :] = block(prev * on(to > 0), nxt * on(to < nrow - 1))

    parity(rows, columns)


def tree_sum(parts):
    parts = [x.astype(jnp.float32) for x in parts]
    while len(parts) > 1:
        parts = [a + b for a, b in zip(parts[::2], parts[1::2])]
    return parts[0]


def sum_kernel(*refs):
    mine_ref, on_ref = refs[-2:]
    half = on_ref.shape[0] - 32
    pair = mine_ref.shape[0] - half - 16
    total = tree_sum([x[...] for x in refs[:-2]])
    mine_ref[...] = total
    edge = jnp.concatenate([total[0:8], total[pair - 8 : pair]], axis=0)
    on_ref[...] = jnp.concatenate([total[pair:], edge], axis=0).astype(on_ref.dtype)


def last_kernel(nz, *refs):
    parts, out_ref = refs[:-1], refs[-1]
    half = parts[0].shape[0] - 32
    z = lax.axis_index("col") // 2
    total = tree_sum([x[0 : half + 16, :] for x in parts])
    out_ref[0:half, :] = total[0:half]
    spot = lax.broadcasted_iota(jnp.int32, (16, total.shape[1]), 0)
    prev = jnp.where(z == 0, total[half : half + 1], 0.0)
    nxt = jnp.where(z == nz - 1, total[half + 8 : half + 9], 0.0)
    for k in range(1, nz):
        edge = parts[k][half + 16 :, :].astype(jnp.float32)
        to = jnp.bitwise_xor(z, k)
        prev = jnp.where(to == z - 1, edge[15:16], prev)
        nxt = jnp.where(to == z + 1, edge[0:1], nxt)
    out_ref[half:, :] = jnp.where(spot == 0, prev, jnp.where(spot == 8, nxt, 0.0))


def back(dlatent, weight_ref):
    dagg = lax.dot_general(
        dlatent.astype(jnp.bfloat16), weight_ref[...], (((1,), (1,)), ((), ())),
        preferred_element_type=jnp.float32,
    )
    return dagg.astype(jnp.bfloat16).astype(jnp.float32)


def inner_kernel(mine_ref, theirs_ref, weight_ref, body_ref, sib_ref, out_ref):
    shard = out_ref.shape[0]
    pair = 2 * shard
    real = jnp.float32
    link = body_ref[shard:, :].astype(real)
    dagg = back(mine_ref[0:pair, :] + theirs_ref[0:pair, :], weight_ref)
    none = jnp.zeros((1, dagg.shape[1]), real)

    def even():
        nxt = sib_ref[shard : shard + 16, :].astype(real)[0:1] * dagg[shard : shard + 1]
        out_ref[...] = stencil(dagg[0:shard], link, none, nxt)

    def odd():
        out_ref[...] = stencil(dagg[shard:], link, dagg[shard - 1 : shard], none)

    parity(even, odd)


def final_kernel(
    scale, inner_ref, mine_ref, theirs_ref, last_ref, got_ref, weight_ref, body_ref, far_ref,
    features_ref, grad_ref,
):
    half = last_ref.shape[0] - 16
    shard = inner_ref.shape[0]
    at = mine_ref.shape[0] - 16
    real = jnp.float32
    kind = features_ref.dtype
    spot = lax.broadcasted_iota(jnp.int32, (16, inner_ref.shape[1]), 0)

    def even():
        near = back(mine_ref[at:, :] + got_ref[half:, :], weight_ref)[0:1]
        near = near * body_ref[shard : shard + 16, :].astype(real)[0:1]
        head = inner_ref[0:16, :] + jnp.where(spot == 0, 0.25 * near, 0.0)
        features_ref[0:16, :] = head.astype(kind)
        features_ref[16:, :] = inner_ref[16:, :].astype(kind)
        grad_ref[0:half, :] = last_ref[0:half, :] * scale
        grad_ref[half:, :] = got_ref[0:half, :] * scale

    def odd():
        near = back(theirs_ref[at:, :] + last_ref[half:, :], weight_ref)[8:9]
        near = near * far_ref[...].astype(real)[1:2]
        foot = inner_ref[shard - 16 :, :] + jnp.where(spot == 15, 0.25 * near, 0.0)
        features_ref[0 : shard - 16, :] = inner_ref[0 : shard - 16, :].astype(kind)
        features_ref[shard - 16 :, :] = foot.astype(kind)
        grad_ref[0:half, :] = got_ref[0:half, :] * scale
        grad_ref[half:, :] = last_ref[0:half, :] * scale

    parity(even, odd)


def call(kernel, outs, operands, mib, specs=None):
    return pl.pallas_call(
        kernel,
        out_shape=outs,
        in_specs=specs or [VMEM] * len(operands),
        out_specs=jax.tree.map(lambda _: VMEM, outs),
        compiler_params=params(mib),
    )(*operands)


def local(features, weight, cuts, pos_rows, pos_cols, pos_keys, pos_count, neg_rows, neg_cols):
    shard, width = features.shape
    ncol = lax.axis_size("col")
    nrow = lax.axis_size("row")
    nz = ncol // 2
    per = shard // BLOCK
    steps = max(nz, nrow)
    bf16, real = jnp.bfloat16, jnp.float32
    shape = jax.ShapeDtypeStruct

    at = Slots(pos_rows.shape[2], neg_rows.shape[2])
    slots = (pos_rows, pos_cols, pos_keys, neg_rows, neg_cols)
    body, meta, ends = bodies(at, features, slots, cuts)
    far = swap_next(ends)
    cols = nrow * per
    pieces = max(1, ncol * per * cols // CHUNK_CELLS)
    blocks = ncol * per // pieces
    bounds = BOUNDS if pieces == 1 else (0, 64)
    found = [
        targets(at, k * blocks, blocks, cols, per, 0, bounds, pieces > 1, meta, pos_count, None)
        for k in range(pieces)
    ]
    number = [counts(at, k * blocks, blocks, cols, per, meta, pos_count) for k in range(pieces)]
    if pieces == 1:
        far, found, number, body = lax.optimization_barrier((far, found, number, body))
    sib = swap(body, "col", 1)
    sib_far = swap(far, "col", 1)
    pair = call(pair_kernel, shape((2 * shard, width), bf16), (body, sib, far, sib_far), 4)
    recv = [swap_mixed(pair, k) for k in range(steps - 1, 0, -1)][::-1]
    if pieces == 1:
        t = targets(at, 0, blocks, cols, per, 1, bounds, False, meta, pos_count, found[0])
        recv, t = lax.optimization_barrier((recv, t))
        other = [swap(x, "col", 1) for x in recv]
        found = [targets(at, 0, blocks, cols, per, 2, bounds, False, meta, pos_count, t)]
    else:
        other = [swap(x, "col", 1) for x in recv]
    count = nz // pieces
    outs = [
        decode(t, n, weight, pair, recv, other, nz, nrow, k * count, count)
        for k, (t, n) in enumerate(zip(found, number))
    ]
    if pieces == 1:
        drow = outs[0][0]
        early = swap(outs[0][1], "col", 1)
        dcol, late, share = column_parts(nz, outs[0], width)
    else:
        found = [column_parts(count, x, width) for x in outs]
        drow = jnp.concatenate([x[0] for x in outs], axis=0)
        dcol, share = (tree_sum([x[k] for x in found]) for k in (0, 2))
        split = drow.shape[0] // 2
        early = swap(drow[0:split].astype(bf16), "col", 1)
        z = lax.axis_index("col") // 2
        pair_rows = drow.shape[0] // nz
        top = lax.dynamic_slice_in_dim(drow, z * pair_rows, 8)
        bottom = jnp.bitwise_xor(z, nz - 1) * pair_rows + pair_rows - 8
        edge = jnp.concatenate([top, lax.dynamic_slice_in_dim(drow, bottom, 8)], axis=0)
        long = max(dcol.shape[0], split)
        even = jnp.concatenate([dcol, jnp.zeros((long - dcol.shape[0], width), real)], axis=0)
        odd = jnp.concatenate([drow[split:], jnp.zeros((long - split, width), real)], axis=0)
        late = jnp.where(lax.rem(lax.axis_index("col"), 2) == 0, even, odd)
        late = jnp.concatenate([late, share, edge], axis=0).astype(bf16)
    late = swap(late, "col", 1)
    half = weight.shape[0] // 2
    messages = call(
        functools.partial(merge_kernel, nz, nrow),
        [shape((2 * shard + half + 16, width), bf16)] * steps,
        (drow, dcol, share, early, late), 8,
    )
    arrived = [swap_mixed(messages[k], k) for k in range(steps - 1, 0, -1)]
    mine, on = call(
        sum_kernel,
        (shape(messages[0].shape, real), shape((half + 32, width), bf16)),
        [messages[0]] + arrived[::-1], 8,
    )
    theirs = swap(mine, "col", 1)
    arrived = [swap_mixed(on, k, 1) for k in range(steps - 1, 0, -1)]
    last = call(
        functools.partial(last_kernel, nz), shape((half + 16, width), real),
        [on] + arrived[::-1], 4,
    )
    got = swap(last, "col", 1)
    inner_part = call(
        inner_kernel, shape(features.shape, real), (mine, theirs, weight, body, sib), 8
    )
    scale = (shard * ncol * nrow) ** (-0.5)
    return call(
        functools.partial(final_kernel, scale),
        (shape(features.shape, bf16), shape(weight.shape, real)),
        (inner_part, mine, theirs, last, got, weight, body, far), 8,
    )


def solution(mesh):
    placed = (
        P(AXES, None),
        P(),
        P(AXES, None),
        P("row", "col", None),
        P("row", "col", None),
        P("row", "col", None),
        P("row", "col"),
        P("row", "col", None),
        P("row", "col", None),
    )
    return jax.shard_map(
        local, mesh=mesh, in_specs=placed, out_specs=(P(AXES, None), P()), check_vma=False
    )
```
